512 devices in a mesh: seq: 32 (over z, core), head: 16 (over x, y).
Axes of the slice: x: 4, y: 4, z: 16, core: 2. Of those that a mesh axis runs over, the one named last changes fastest.
Arguments:
- conv_output: bfloat16 [4096, 8192], P('seq', 'head'), may hold values from -6 to 6
- output_grad: bfloat16 [4096, 8192], P('seq', 'head'), may hold values from -6 to 6
- write_keys: bfloat16 [4096, 2048], P('seq', 'head'), may hold values from -1.5 to 1.5
- read_queries: bfloat16 [4096, 2048], P('seq', 'head'), may hold values from -1.5 to 1.5
- log_decay: float32 [4096, 128], P('seq', 'head'), may hold values from -0.7 to 0
- step_size: float32 [4096, 128], P('seq', 'head'), may hold values from 0.005 to 0.05
- skip_gain: float32 [128], P('head'), may hold values from 0.5 to 1.5
- conv_weight: float32 [4, 8192], P(None, 'head'), may hold values from -3 to 3
Outputs:
- input_grad: bfloat16 [4096, 8192], P('seq', 'head')
- keys_grad: float32 [4096, 2048], P('seq', 'head')
- queries_grad: float32 [4096, 2048], P('seq', 'head')
- decay_grad: float32 [4096, 128], P('seq', 'head')
- step_grad: float32 [4096, 128], P('seq', 'head')
The draws below stay inside these ranges and needn't reach their ends.
All inputs are finite; a program needn't handle non-finite values.
Results may differ from the reference program's by a relative error of at most 0.0055.
Values may be sent and summed in bfloat16 or wider, within the bound.
A program may use at most 64 MiB of HBM per device.

```python
import math
import jax
import jax.numpy as jnp
from jax import lax

P_SIZE = 64
N = 256
HD = 8
TOK_DEV = 128
HEAD_TOTAL = 128
GROUPS = 8
TOKEN_TOTAL = 4096


def draw_log_decay(key, part):
    random_keys = jax.random.split(key, 7)
    percent = 50
    fast_head = jax.random.randint(random_keys[0], (HEAD_TOTAL,), 0, 100) < percent
    fast_rate = jnp.exp(jax.random.uniform(random_keys[1], (HEAD_TOTAL,), jnp.float32, math.log(1.0 / 50.0), math.log(1.0 / 30.0)))
    slow_rate = jax.random.uniform(random_keys[2], (HEAD_TOTAL,), jnp.float32, 0.1, 0.3) / TOKEN_TOTAL
    head_decay_rate = jnp.where(fast_head, fast_rate, slow_rate)
    blocks = TOKEN_TOTAL // TOK_DEV
    multiplier = jnp.exp(jax.random.uniform(random_keys[3], (blocks, 1, HEAD_TOTAL), jnp.float32, 0.0, math.log(2.0)))
    multiplier = jnp.broadcast_to(multiplier, (blocks, TOK_DEV, HEAD_TOTAL)).reshape(TOKEN_TOTAL, HEAD_TOTAL)
    small_noise = jax.random.uniform(random_keys[4], (TOKEN_TOTAL, HEAD_TOTAL), jnp.float32, 0.5, 1.5)
    spike_mask = jax.random.randint(random_keys[5], (TOKEN_TOTAL, HEAD_TOTAL), 0, max(TOKEN_TOTAL // 2, 1)) == 0
    spike_loss = jax.random.uniform(random_keys[6], (TOKEN_TOTAL, HEAD_TOTAL), jnp.float32, 0.2, 0.4)
    return -head_decay_rate[None, :] * multiplier * small_noise + jnp.where(spike_mask, jnp.log(1.0 - spike_loss), 0.0)


def block_scale(own_key, shape, cuts, smallest, top_value):
    def one(axis_at, parts):
        draws = jax.random.uniform(jax.random.fold_in(jax.random.fold_in(own_key, 6), axis_at), (parts,), jnp.float32, smallest / len(cuts), top_value / len(cuts))
        return jnp.repeat(jnp.exp(draws), shape[axis_at] // parts).reshape((-1,) + (1,) * (len(shape) - axis_at - 1))

    gain = one(*cuts[0])
    for cut in cuts[1:]:
        gain = gain * one(*cut)
    return gain


def noise(stream_key, dims, deviation, most, shards=(), kind=jnp.bfloat16):
    level = block_scale(stream_key, dims, shards, -0.22, 0.18) if shards else 1.0
    array = jax.random.normal(stream_key, dims, jnp.float32) * deviation * level
    return jnp.minimum(jnp.maximum(array, -most), most).astype(kind)


def setup_inputs(seed: int = 0) -> dict:
    splits = jax.random.split(jax.random.key(seed), 9)
    return {
        "conv_output": noise(splits[0], (TOKEN_TOTAL, HEAD_TOTAL * P_SIZE), 1.0, 6.0, ((0, 32), (1, 16))),
        "output_grad": noise(splits[1], (TOKEN_TOTAL, HEAD_TOTAL * P_SIZE), 1.0, 6.0, ((0, 32), (1, 16))),
        "write_keys": noise(splits[2], (TOKEN_TOTAL, GROUPS * N), 0.25, 1.5, ((0, 32), (1, 16))),
        "read_queries": noise(splits[3], (TOKEN_TOTAL, GROUPS * N), 0.25, 1.5, ((0, 32), (1, 16))),
        "log_decay": draw_log_decay(jax.random.fold_in(splits[8], 71), 0),
        "step_size": jnp.clip(jnp.exp(math.log(0.05) - 2.3025851 * jax.random.uniform(splits[5], (TOKEN_TOTAL, HEAD_TOTAL), jnp.float32) ** block_scale(splits[5], (TOKEN_TOTAL, HEAD_TOTAL), ((0, 32), (1, 16)), -0.2, 0.2)), 0.005, 0.05),
        "skip_gain": jnp.clip(0.5 + 1.0 * jax.random.uniform(splits[6], (HEAD_TOTAL,), jnp.float32) ** block_scale(splits[6], (HEAD_TOTAL,), ((0, 16),), -0.2, 0.2), 0.5, 1.5),
        "conv_weight": noise(splits[7], (4, HEAD_TOTAL * P_SIZE), 0.5, 3.0, ((1, 16),), jnp.float32),
    }


precise = lax.Precision.HIGHEST

def group_forward(conv_part, keys_part, queries_part, decay_part, step_part, skip_part, block):
    count = decay_part.shape[1]
    values = jax.nn.silu(conv_part).reshape(-1, block, count, P_SIZE)
    keys_blocks = keys_part.reshape(-1, block, N)
    query_blocks = queries_part.reshape(-1, block, N)
    cumulative = jnp.cumsum(decay_part.reshape(-1, block, count), axis=1)
    step_blocks = step_part.reshape(-1, block, count)
    row_ids = lax.broadcasted_iota(jnp.int32, (block, block), 0)
    col_ids = lax.broadcasted_iota(jnp.int32, (block, block), 1)
    causal = row_ids >= col_ids

    def advance(state, inputs):
        block_values, block_keys, block_queries, block_cum, block_step = inputs
        scores = jnp.dot(block_queries, block_keys.T, precision=precise, preferred_element_type=jnp.float32)
        log_gap = jnp.where(causal[:, :, None], block_cum[:, None, :] - block_cum[None, :, :], -1e+30)
        mixing = jnp.exp(log_gap) * scores[:, :, None] * block_step[None, :, :]
        inside = jnp.einsum('tsh,shp->thp', mixing, block_values, precision=precise)
        carried = jnp.exp(block_cum)[:, :, None] * jnp.einsum('tn,hnp->thp', block_queries, state, precision=precise)
        outputs = inside + carried + skip_part[None, :, None] * block_values
        to_end = jnp.exp(block_cum[-1][None, :] - block_cum) * block_step
        written = jnp.einsum('sn,shp->hnp', block_keys, block_values * to_end[:, :, None], precision=precise)
        new_state = jnp.exp(block_cum[-1])[:, None, None] * state + written
        return (new_state, outputs)
    initial = jnp.zeros((count, N, P_SIZE), conv_part.dtype)
    _, outputs = lax.scan(advance, initial, (values, keys_blocks, query_blocks, cumulative, step_blocks))
    return outputs.reshape(TOKEN_TOTAL, count * P_SIZE)

def reference(conv_output, output_grad, write_keys, read_queries, log_decay, step_size, skip_gain, conv_weight):
    group_heads = 2 * HD
    groups = HEAD_TOTAL // group_heads
    block = math.gcd(TOKEN_TOTAL, 64)
    conv_all = conv_output.astype(jnp.float32).reshape(TOKEN_TOTAL, groups, group_heads * P_SIZE).transpose(1, 0, 2)
    grads_all = output_grad.astype(jnp.float32).reshape(TOKEN_TOTAL, groups, group_heads * P_SIZE).transpose(1, 0, 2)
    keys_all = write_keys.astype(jnp.float32).reshape(TOKEN_TOTAL, groups, N).transpose(1, 0, 2)
    queries_all = read_queries.astype(jnp.float32).reshape(TOKEN_TOTAL, groups, N).transpose(1, 0, 2)
    decay_all = log_decay.reshape(TOKEN_TOTAL, groups, group_heads).transpose(1, 0, 2)
    step_all = step_size.reshape(TOKEN_TOTAL, groups, group_heads).transpose(1, 0, 2)
    skip_all = skip_gain.reshape(groups, group_heads)
    weight_all = conv_weight.reshape(4, groups, group_heads * P_SIZE).transpose(1, 0, 2)

    def one_group(inputs):
        conv_part, grad_part, keys_part, queries_part, decay_part, step_part, skip_part, weight_part = inputs

        def forward(conv_in, keys_in, queries_in, decay_in, step_in):
            return group_forward(conv_in, keys_in, queries_in, decay_in, step_in, skip_part, block)
        _, pullback = jax.vjp(forward, conv_part, keys_part, queries_part, decay_part, step_part)
        conv_grad, keys_grad, queries_grad, decay_grad, step_grad = pullback(grad_part)
        extended = jnp.concatenate([conv_grad, jnp.zeros((3, conv_grad.shape[1]), conv_grad.dtype)], 0)
        input_grad = jnp.zeros_like(conv_grad)
        for offset in range(4):
            input_grad = input_grad + weight_part[offset][None, :] * extended[3 - offset:3 - offset + TOKEN_TOTAL]
        return (input_grad.astype(jnp.bfloat16), keys_grad, queries_grad, decay_grad, step_grad)
    results = lax.map(one_group, (conv_all, grads_all, keys_all, queries_all, decay_all, step_all, skip_all, weight_all))
    input_grad = results[0].transpose(1, 0, 2).reshape(TOKEN_TOTAL, HEAD_TOTAL * P_SIZE)
    keys_grad = results[1].transpose(1, 0, 2).reshape(TOKEN_TOTAL, groups * N)
    queries_grad = results[2].transpose(1, 0, 2).reshape(TOKEN_TOTAL, groups * N)
    decay_grad = results[3].transpose(1, 0, 2).reshape(TOKEN_TOTAL, HEAD_TOTAL)
    step_grad = results[4].transpose(1, 0, 2).reshape(TOKEN_TOTAL, HEAD_TOTAL)
    return (input_grad, keys_grad, queries_grad, decay_grad, step_grad)
```

```python
import functools

import jax
import jax.numpy as jnp
from jax import lax
from jax.experimental import pallas as pl
from jax.experimental.pallas import tpu as pltpu
from jax.sharding import PartitionSpec as P

MESH = pl.DeviceIdType.MESH
F32 = jnp.float32
BF16 = jnp.bfloat16
LEN = 128
WIDTH = 512
HEADS = 8
HALF = 128
STATE = 256
CHUNK = 32
CHUNKS = STATE // CHUNK


def dot(a, b):
    return lax.dot_general(a, b, (((1,), (0,)), ((), ())), preferred_element_type=F32)


def dot_t(a, b):
    return lax.dot_general(a, b, (((1,), (1,)), ((), ())), preferred_element_type=F32)


def split2(x):
    hi = x.astype(BF16)
    return hi, (x - hi.astype(F32)).astype(BF16)


def split3(x):
    hi = x.astype(BF16)
    rest = x - hi.astype(F32)
    mid = rest.astype(BF16)
    return hi, mid, (rest - mid.astype(F32)).astype(BF16)


def iota(shape, axis):
    return lax.broadcasted_iota(jnp.int32, shape, axis)


def flag(cond):
    return cond.astype(F32).astype(BF16)


def kernel(
    n_seq, conv_ref, og_ref, k_ref, q_ref, ld_ref, ss_ref, skip_ref, cw_ref,
    igrad_ref, kgrad_ref, qgrad_ref, dgrad_ref, sgrad_ref,
    pad_ld, pad_ss, pad_skip, col_s, row_s, kp, qp, vhi, vlo, vals, dsilu, tsx, whi, wlo, shi, slo, within, wsum,
    lme, lsend, lother, tt, tsend, tlow, uu, dme8, doth8, dchip8, dlow8, xin, xsend, ebuf, epart,
    ext, kpart, qpart, krecv, qrecv,
    kq_ss, kq_rs, d_ss, d_rs, l_ss, l_rs, t_ss, t_rs, x_ss, x2_ss, x_rs, e_ss, e_rs, f_ss, f_rs, c_ss, c_rs,
):
    seq = lax.axis_index("seq")
    head = lax.axis_index("head")
    core = lax.rem(seq, 2)
    chip = seq // 2
    chips = n_seq // 2
    pos = jnp.where(core == 0, chip, chips - 1 - chip)
    group = pos // 2
    high = lax.rem(pos, 2) == 1
    low = lax.rem(pos, 2) == 0
    opens = group == 0
    sends_on = jnp.logical_and(high, group < chips // 2 - 1)
    step1 = jnp.where(core == 0, 2, n_seq - 2)
    step2 = jnp.where(core == 0, 4, n_seq - 4)

    def at(s):
        return (lax.rem(s, n_seq), head)

    next1 = at(seq + step1)
    next2 = at(seq + step2)
    other_core = at(seq + 1 - 2 * core)
    before = at(seq + n_seq - 1)
    after_or_before = at(seq + jnp.where(core == 0, n_seq - 1, 1))
    partner = (seq, head + 1 - 2 * lax.rem(head, 2))

    barrier = pltpu.get_barrier_semaphore()
    greeted = (
        at(seq + 2), at(seq + n_seq - 2), at(seq + 4), at(seq + n_seq - 4), other_core, after_or_before, partner,
    )
    for peer in greeted:
        pl.semaphore_signal(barrier, inc=1, device_id=peer, device_id_type=MESH)

    def remote(src, dst, ss, rs, peer):
        return pltpu.make_async_remote_copy(
            src_ref=src, dst_ref=dst, send_sem=ss, recv_sem=rs, device_id=peer, device_id_type=MESH
        )

    pad_ld[...] = jnp.zeros((LEN, LEN), F32)
    pad_ss[...] = jnp.zeros((LEN, LEN), F32)
    pad_skip[...] = jnp.zeros((8, LEN), F32)
    pad_ld[:, 0:HEADS] = ld_ref[...]
    pad_ss[:, 0:HEADS] = ss_ref[...]
    pad_skip[0:1, 0:HEADS] = skip_ref[...]
    rows = iota((LEN, LEN), 0)
    cols = iota((LEN, LEN), 1)
    lower = flag(rows >= cols)
    spread = flag(iota((LEN, WIDTH), 0) == iota((LEN, WIDTH), 1) // 64)
    gather = flag(iota((WIDTH, LEN), 0) // 64 == iota((WIDTH, LEN), 1))

    def expand(x):
        hi, lo = split2(x)
        return dot(hi, spread) + dot(lo, spread)

    def by_head(x):
        hi, lo = split2(x)
        return dot(hi, gather) + dot(lo, gather)

    hi, mid, lo = split3(pad_ld[...])
    cum = dot(lower, hi) + (dot(lower, mid) + dot(lower, lo))
    step = pad_ss[...]
    from_start = jnp.exp(cum)
    total = cum[LEN - 1 : LEN, :]
    to_end = jnp.exp(total - cum)
    fsx = expand(from_start)
    tsx[...] = expand(to_end * step)
    d_me = fsx[LEN - 1 : LEN, :]
    dme8[...] = jnp.broadcast_to(d_me, (8, WIDTH))

    pl.semaphore_wait(barrier, len(greeted))
    k_copy = remote(k_ref, kp, kq_ss.at[0], kq_rs.at[0], partner)
    q_copy = remote(q_ref, qp, kq_ss.at[1], kq_rs.at[1], partner)
    k_copy.start()
    q_copy.start()
    d_copy = remote(dme8, doth8, d_ss.at[0], d_rs.at[0], other_core)
    d_copy.start()

    preact = conv_ref[...].astype(F32)
    sig = 1.0 / (1.0 + jnp.exp(-preact))
    value = preact * sig
    vals[...] = value
    vhi[...], vlo[...] = split2(value)
    dsilu[...] = sig * (1.0 + preact * (1.0 - sig))
    whi[...], wlo[...] = split2(value * tsx[...])
    shi[...], slo[...] = split2(og_ref[...].astype(F32) * fsx)

    forward = core == 0

    def turned(x):
        return x.astype(F32).T.astype(BF16)

    def local_half(at_row, kk, qq, half):
        kt, qt = turned(kk), turned(qq)
        wh, wl, sh, sl = whi[...], wlo[...], shi[...], slo[...]
        mine, other = jnp.where(forward, kt, qt), jnp.where(forward, qt, kt)
        lsend[at_row : at_row + HALF, :] = dot(other, jnp.where(forward, sh, wh)) + dot(
            other, jnp.where(forward, sl, wl)
        )
        part = pl.ds(at_row, HALF)
        remote(lsend.at[part], lother.at[part], l_ss.at[half], l_rs.at[half], other_core).start()
        lme[at_row : at_row + HALF, :] = dot(mine, jnp.where(forward, wh, sh)) + dot(
            mine, jnp.where(forward, wl, sl)
        )

    local_half(0, k_ref[...], q_ref[...], 0)
    k_copy.wait_recv()
    q_copy.wait_recv()
    local_half(HALF, kp[...], qp[...], 1)

    d_copy.wait_recv()
    d_me8 = dme8[...]
    d_oth8 = doth8[...]
    dchip8[...] = d_me8 * d_oth8

    @pl.when(low)
    def _():
        remote(dchip8, dlow8, d_ss.at[1], d_rs.at[1], next1).start()

    def chip_half(half):
        at_row = half * HALF
        part = pl.ds(at_row, HALF)
        remote(lsend.at[part], lother.at[part], l_ss.at[half], l_rs.at[half], other_core).wait_recv()
        sl = slice(at_row, at_row + HALF)
        whole = d_oth8[0:1, :] * lme[sl, :] + lother[sl, :]
        tt[sl, :] = whole

        @pl.when(low)
        def _():
            tsend[sl, :] = whole
            remote(tsend.at[part], tlow.at[part], t_ss.at[half], t_rs.at[half], next1).start()

    chip_half(0)
    chip_half(1)

    @pl.when(low)
    def _():
        tlow[...] = jnp.zeros((STATE, WIDTH), F32)
        dlow8[...] = jnp.ones((8, WIDTH), F32)

    @pl.when(opens)
    def _():
        xin[...] = jnp.zeros((STATE, WIDTH), F32)

    def group_totals():
        @pl.when(high)
        def _():
            remote(dchip8, dlow8, d_ss.at[1], d_rs.at[1], next1).wait_recv()
            for half in range(2):
                part = pl.ds(half * HALF, HALF)
                sl = slice(half * HALF, half * HALF + HALF)
                remote(tsend.at[part], tlow.at[part], t_ss.at[half], t_rs.at[half], next1).wait_recv()
                uu[sl, :] = dchip8[0:1, :] * tlow[sl, :] + tt[sl, :]

    def x_copy(c, far):
        part = pl.ds(c * CHUNK, CHUNK)
        return remote(
            xsend.at[part], xin.at[part], (x2_ss if far else x_ss).at[c], x_rs.at[c], next2 if far else next1
        )

    def e_copy(c):
        part = pl.ds(c * CHUNK, CHUNK)
        return remote(epart.at[part], ebuf.at[core, part], e_ss.at[c], e_rs.at[c], other_core)

    def chain():
        group_totals()
        a = dlow8[0:1, :]
        dd = dchip8[0:1, :] * a
        dm = dme8[0:1, :]
        for c in range(CHUNKS):
            sl = slice(c * CHUNK, c * CHUNK + CHUNK)

            @pl.when(jnp.logical_not(opens))
            def _():
                x_copy(c, False).wait_recv()

            x = xin[sl, :]

            @pl.when(sends_on)
            def _():
                xsend[sl, :] = dd * x + uu[sl, :]
                x_copy(c, True).start()
                x_copy(c, False).start()

            em = a * x + tlow[sl, :]
            ebuf[core, sl, :] = em
            epart[sl, :] = dm * em + lme[sl, :]
            e_copy(c).start()

    def inside():
        scores = dot_t(k_ref[...], q_ref[...]) + dot_t(kp[...], qp[...])
        causal = rows <= cols
        cum_t = cum.T
        left = iota((LEN, LEN), 1) < 64
        col_s[...] = jnp.zeros((LEN, LEN), F32)
        row_s[...] = jnp.zeros((LEN, LEN), F32)
        weights = jnp.zeros((LEN, LEN), F32)
        for j in range(HEADS // 2):
            lanes = slice(j * 128, j * 128 + 128)
            ogb = og_ref[:, lanes]
            vh, vl = vhi[:, lanes], vlo[:, lanes]
            halves = []
            for e in range(2):
                h = 2 * j + e
                own = left if e == 0 else jnp.logical_not(left)
                none = jnp.zeros_like(vh)
                pd = dot_t(jnp.where(own, vh, none), ogb) + dot_t(jnp.where(own, vl, none), ogb)
                gap = cum_t[h : h + 1, :] - cum[:, h : h + 1]
                dm = jnp.exp(jnp.where(causal, gap, -1e30))
                st = step[:, h : h + 1]
                a = dm * scores
                weights = weights + dm * pd * st
                eff = a * pd
                a_st = a * st
                col_s[:, h : h + 1] = jnp.sum(eff, axis=1, keepdims=True)
                row_s[h : h + 1, :] = jnp.sum(eff * st, axis=0, keepdims=True)
                halves.append(dot(a_st.astype(BF16), ogb))
            within[:, lanes] = jnp.where(left, halves[0], halves[1])
        wsum[...] = weights
        sk_hi, sk_lo = split2(pad_skip[...])
        skip_row = (dot(sk_hi, spread) + dot(sk_lo, spread))[0:1, :]
        within[...] = within[...] + skip_row * og_ref[...].astype(F32)

    def turn(i, carry):
        first = i == 0

        @pl.when(jnp.logical_xor(first, opens))
        def _():
            inside()

        @pl.when(jnp.logical_not(jnp.logical_xor(first, opens)))
        def _():
            chain()

        return carry

    lax.fori_loop(0, 2, turn, 0)

    for c in range(CHUNKS):
        e_copy(c).wait_recv()

    entering = ebuf[0]
    arriving = ebuf[1]
    w = wsum[...]
    wm, wm_t = split2(w), split2(w.T)
    wt = (whi[...], wlo[...])
    sd = (shi[...], slo[...])

    def own_half(x):
        return split2(x[0:HALF, :])

    def far_half(x):
        return split2(x[HALF:, :])

    def twice(a, b):
        return dot(a[0], b) + dot(a[1], b)

    def thrice_t(a, b):
        return dot_t(a[0], b[0]) + (dot_t(a[0], b[1]) + dot_t(a[1], b[0]))

    def left(a, b):
        return dot(a, b[0]) + dot(a, b[1])

    a_far = far_half(arriving)
    kpart[...] = (twice(wm, qp[...]) + thrice_t(wt, a_far)).astype(BF16)
    k_back = remote(kpart, krecv, f_ss.at[0], f_rs.at[0], partner)
    k_back.start()
    e_far = far_half(entering)
    qpart[...] = (twice(wm_t, kp[...]) + thrice_t(sd, e_far)).astype(BF16)
    q_back = remote(qpart, qrecv, f_ss.at[1], f_rs.at[1], partner)
    q_back.start()

    a_own, e_own = own_half(arriving), own_half(entering)
    into = left(k_ref[...], a_own) + left(kp[...], a_far)
    ext[0:LEN, :] = (within[...] + tsx[...] * into) * dsilu[...]
    c_copy = remote(ext.at[pl.ds(0, 8)], ext.at[pl.ds(LEN, 8)], c_ss.at[0], c_rs.at[0], before)

    @pl.when(seq > 0)
    def _():
        c_copy.start()

    @pl.when(seq == n_seq - 1)
    def _():
        ext[LEN : LEN + 8, :] = jnp.zeros((8, WIDTH), F32)

    k_own = twice(wm, q_ref[...]) + thrice_t(wt, a_own)
    q_own = twice(wm_t, k_ref[...]) + thrice_t(sd, e_own)
    out_of = left(q_ref[...], e_own) + left(qp[...], e_far)
    carried = by_head(vals[...] * into)
    read = by_head(og_ref[...].astype(F32) * out_of)
    cross = jnp.sum(entering * arriving, axis=0, keepdims=True)
    cross = by_head(jnp.broadcast_to(cross, (8, WIDTH)))[0:1, :]
    col = col_s[...]
    row = row_s[...].T
    sgrad_ref[...] = (col + to_end * carried)[:, 0:HEADS]
    later = row - col * step + from_start * read
    earlier = to_end * step * carried
    upper = flag(rows <= cols)
    strict = flag(rows > cols)
    lh, ll = split2(later)
    eh, el = split2(earlier)
    decay = dot(upper, lh) + dot(upper, ll) + dot(strict, eh) + dot(strict, el)
    decay = decay + jnp.exp(total) * cross
    dgrad_ref[...] = decay[:, 0:HEADS]

    k_back.wait_recv()
    kgrad_ref[...] = k_own + krecv[...].astype(F32)
    q_back.wait_recv()
    qgrad_ref[...] = q_own + qrecv[...].astype(F32)

    @pl.when(seq < n_seq - 1)
    def _():
        c_copy.wait_recv()

    acc = cw_ref[3:4, :] * ext[0:LEN, :]
    for tap in range(3):
        acc = acc + cw_ref[tap : tap + 1, :] * ext[3 - tap : 3 - tap + LEN, :]
    igrad_ref[...] = acc.astype(BF16)

    k_copy.wait_send()
    q_copy.wait_send()
    d_copy.wait_send()
    for half in range(2):
        part = pl.ds(half * HALF, HALF)
        remote(lsend.at[part], lother.at[part], l_ss.at[half], l_rs.at[half], other_core).wait_send()

    @pl.when(low)
    def _():
        remote(dchip8, dlow8, d_ss.at[1], d_rs.at[1], next1).wait_send()
        for half in range(2):
            part = pl.ds(half * HALF, HALF)
            remote(tsend.at[part], tlow.at[part], t_ss.at[half], t_rs.at[half], next1).wait_send()

    @pl.when(sends_on)
    def _():
        for c in range(CHUNKS):
            x_copy(c, True).wait_send()
            x_copy(c, False).wait_send()

    for c in range(CHUNKS):
        e_copy(c).wait_send()
    k_back.wait_send()
    q_back.wait_send()

    @pl.when(seq > 0)
    def _():
        c_copy.wait_send()


def body(n_seq, conv_output, output_grad, write_keys, read_queries, log_decay, step_size, skip_gain, conv_weight):
    shape = jax.ShapeDtypeStruct
    vmem = pltpu.VMEM
    dma = pltpu.SemaphoreType.DMA
    big = (STATE, WIDTH)
    tok = (LEN, WIDTH)
    sq = (LEN, LEN)
    return pl.pallas_call(
        functools.partial(kernel, n_seq),
        out_shape=(
            shape(tok, BF16), shape(sq, F32), shape(sq, F32), shape((LEN, HEADS), F32), shape((LEN, HEADS), F32),
        ),
        in_specs=[pl.BlockSpec(memory_space=vmem)] * 8,
        out_specs=(pl.BlockSpec(memory_space=vmem),) * 5,
        scratch_shapes=[
            vmem(sq, F32), vmem(sq, F32), vmem((8, LEN), F32), vmem(sq, F32), vmem(sq, F32),
            vmem(sq, BF16), vmem(sq, BF16), vmem(tok, BF16), vmem(tok, BF16), vmem(tok, F32), vmem(tok, F32),
            vmem(tok, F32), vmem(tok, BF16), vmem(tok, BF16), vmem(tok, BF16), vmem(tok, BF16),
            vmem(tok, F32), vmem(sq, F32),
            vmem(big, F32), vmem(big, F32), vmem(big, F32),
            vmem(big, F32), vmem(big, F32), vmem(big, F32), vmem(big, F32),
            vmem((8, WIDTH), F32), vmem((8, WIDTH), F32), vmem((8, WIDTH), F32), vmem((8, WIDTH), F32),
            vmem(big, F32), vmem(big, F32), vmem((2,) + big, F32), vmem(big, F32),
            vmem((LEN + 8, WIDTH), F32), vmem(sq, BF16), vmem(sq, BF16), vmem(sq, BF16), vmem(sq, BF16),
            dma((2,)), dma((2,)), dma((2,)), dma((2,)), dma((2,)), dma((2,)), dma((2,)), dma((2,)),
            dma((CHUNKS,)), dma((CHUNKS,)), dma((CHUNKS,)), dma((CHUNKS,)), dma((CHUNKS,)),
            dma((2,)), dma((2,)), dma((1,)), dma((1,)),
        ],
        compiler_params=pltpu.CompilerParams(
            collective_id=0, has_side_effects=True, vmem_limit_bytes=40 * 1024 * 1024
        ),
        cost_estimate=pl.CostEstimate(flops=300_000_000, bytes_accessed=1_000_000, transcendentals=300_000),
    )(
        conv_output, output_grad, write_keys, read_queries, log_decay, step_size,
        skip_gain.reshape(1, HEADS), conv_weight,
    )


def solution(mesh):
    spec = P("seq", "head")
    return jax.shard_map(
        functools.partial(body, mesh.shape["seq"]),
        mesh=mesh,
        in_specs=(spec, spec, spec, spec, spec, spec, P("head"), P(None, "head")),
        out_specs=(spec,) * 5,
        check_vma=False,
    )
```

```python
import functools

import jax
import jax.numpy as jnp
from jax import lax
from jax.experimental import pallas as pl
from jax.experimental.pallas import tpu as pltpu
from jax.sharding import PartitionSpec as P

MESH = pl.DeviceIdType.MESH
F32 = jnp.float32
BF16 = jnp.bfloat16
LEN = 128
WIDTH = 512
HEADS = 8
HALF = 128
VMEM_BYTES = 58000 * 1024
STATE = 256
CHUNK = 16
CHUNKS = STATE // CHUNK
NEAR_LAG = 1


def dot(a, b):
    return lax.dot_general(a, b, (((1,), (0,)), ((), ())), preferred_element_type=F32)


def dot_t(a, b):
    return lax.dot_general(a, b, (((1,), (1,)), ((), ())), preferred_element_type=F32)


def split2(x):
    hi = x.astype(BF16)
    return hi, (x - hi.astype(F32)).astype(BF16)


def split3(x):
    hi = x.astype(BF16)
    rest = x - hi.astype(F32)
    mid = rest.astype(BF16)
    return hi, mid, (rest - mid.astype(F32)).astype(BF16)


def iota(shape, axis):
    return lax.broadcasted_iota(jnp.int32, shape, axis)


def flag(cond):
    return cond.astype(F32).astype(BF16)


def kernel(
    n_seq, conv_hbm, og_hbm, k_hbm, q_hbm, ld_hbm, ss_hbm, skip_hbm, cw_hbm,
    igrad_ref, kgrad_ref, qgrad_ref, dgrad_ref, sgrad_ref,
    conv_ref, og_ref, k_ref, q_ref, ld_ref, ss_ref, skip_ref, cw_ref,
    pack, col_s, row_s, kp, qp, vhi, vlo, vals, dsilu, tsx, whi, wlo, shi, slo, within,
    k_in, q_in, k_far, q_far, read_s, carried_s,
    lme, lsend, lother, tt, tlow, dme8, doth8, dchip8, dlow8, xin, xsend, xnear, xnsend, ebuf, epart,
    ext, kpart, qpart, krecv, qrecv,
    in_s, kq_ss, kq_rs, d_ss, d_rs, l_ss, l_rs, t_ss, t_rs, x_ss, x2_ss, x_rs, n_rs, e_ss, e_rs, f_ss, f_rs, c_ss, c_rs,
):
    seq = lax.axis_index("seq")
    head = lax.axis_index("head")
    core = lax.rem(seq, 2)
    chip = seq // 2
    chips = n_seq // 2
    pos = jnp.where(core == 0, chip, chips - 1 - chip)
    group = pos // 2
    high = lax.rem(pos, 2) == 1
    low = lax.rem(pos, 2) == 0
    opens = group == 0
    late = group >= chips // 4
    sends_on = jnp.logical_and(high, group < chips // 2 - 1)
    step1 = jnp.where(core == 0, 2, n_seq - 2)
    step2 = jnp.where(core == 0, 4, n_seq - 4)

    def at(s):
        return (lax.rem(s, n_seq), head)

    next1 = at(seq + step1)
    next2 = at(seq + step2)
    other_core = at(seq + 1 - 2 * core)
    before = at(seq + n_seq - 1)
    after_or_before = at(seq + jnp.where(core == 0, n_seq - 1, 1))
    partner = (seq, head + 1 - 2 * lax.rem(head, 2))

    barrier = pltpu.get_barrier_semaphore()
    greeted = (
        at(seq + 2), at(seq + n_seq - 2), at(seq + 4), at(seq + n_seq - 4), other_core, after_or_before, partner,
    )
    for peer in greeted:
        pl.semaphore_signal(barrier, inc=1, device_id=peer, device_id_type=MESH)

    moves = [
        pltpu.make_async_copy(src, dst, in_s.at[n])
        for n, (src, dst) in enumerate((
            (ld_hbm, ld_ref), (ss_hbm, ss_ref), (conv_hbm, conv_ref), (og_hbm, og_ref),
            (k_hbm, k_ref), (q_hbm, q_ref), (skip_hbm, skip_ref), (cw_hbm, cw_ref),
        ))
    ]
    for move in moves:
        move.start()

    def remote(src, dst, ss, rs, peer):
        return pltpu.make_async_remote_copy(
            src_ref=src, dst_ref=dst, send_sem=ss, recv_sem=rs, device_id=peer, device_id_type=MESH
        )

    rows = iota((LEN, LEN), 0)
    cols = iota((LEN, LEN), 1)
    upto = flag(rows <= cols)
    pack[...] = jnp.zeros((LEN, LEN), F32)
    heads_rows = flag(iota((HEADS, WIDTH), 0) == iota((HEADS, WIDTH), 1) // 64)

    def spread(base):
        return flag(iota((LEN, WIDTH), 0) - base == iota((LEN, WIDTH), 1) // 64)

    def by_head(x):
        hi, lo = split2(x)
        return dot_t(heads_rows, hi) + dot_t(heads_rows, lo)

    moves[0].wait()
    moves[1].wait()
    hi, mid, lo = split3(ld_ref[...])
    cum_t = dot(hi, upto) + (dot(mid, upto) + dot(lo, upto))
    step_t = ss_ref[...]
    total = cum_t[:, LEN - 1 : LEN]
    from_start = jnp.exp(cum_t)
    to_end = jnp.exp(total - cum_t)
    pack[0:8, :] = cum_t
    pack[8:16, :] = step_t
    pack[16:24, :] = from_start
    pack[24:32, :] = to_end * step_t
    columns = pack[...].T
    c_hi, c_lo = split2(columns)
    fs_sel, ts_sel = spread(16), spread(24)
    fsx = dot(c_hi, fs_sel) + dot(c_lo, fs_sel)
    tsx[...] = dot(c_hi, ts_sel) + dot(c_lo, ts_sel)
    dme8[...] = jnp.broadcast_to(fsx[LEN - 1 : LEN, :], (8, WIDTH))

    pl.semaphore_wait(barrier, len(greeted))
    k_copy = remote(k_hbm, kp, kq_ss.at[0], kq_rs.at[0], partner)
    q_copy = remote(q_hbm, qp, kq_ss.at[1], kq_rs.at[1], partner)
    k_copy.start()
    q_copy.start()
    d_copy = remote(dme8, doth8, d_ss.at[0], d_rs.at[0], other_core)
    d_copy.start()

    moves[2].wait()
    preact = conv_ref[...].astype(F32)
    sig = 1.0 / (1.0 + jnp.exp(-preact))
    value = preact * sig
    vals[...] = value
    vhi[...], vlo[...] = split2(value)
    dsilu[...] = sig * (1.0 + preact * (1.0 - sig))
    whi[...], wlo[...] = split2(value * tsx[...])
    moves[3].wait()
    shi[...], slo[...] = split2(og_ref[...].astype(F32) * fsx)

    forward = core == 0

    def turned(x):
        return x.astype(F32).T.astype(BF16)

    def l_copy(half):
        part = pl.ds(half * HALF, HALF)
        return remote(lsend.at[part], lother.at[part], l_ss.at[half], l_rs.at[half], other_core)

    def local_half(half, kk, qq):
        sl = slice(half * HALF, half * HALF + HALF)
        kt, qt = turned(kk), turned(qq)
        wh, wl, sh, slw = whi[...], wlo[...], shi[...], slo[...]
        mine, other = jnp.where(forward, kt, qt), jnp.where(forward, qt, kt)
        lsend[sl, :] = dot(other, jnp.where(forward, sh, wh)) + dot(other, jnp.where(forward, slw, wl))
        l_copy(half).start()
        lme[sl, :] = dot(mine, jnp.where(forward, wh, sh)) + dot(mine, jnp.where(forward, wl, slw))

    moves[4].wait()
    moves[5].wait()
    local_half(0, k_ref[...], q_ref[...])
    k_copy.wait_recv()
    q_copy.wait_recv()
    local_half(1, kp[...], qp[...])
    moves[6].wait()
    moves[7].wait()

    d_copy.wait_recv()
    dchip8[...] = dme8[...] * doth8[...]

    def dt_copy():
        return remote(dchip8, dlow8, d_ss.at[1], d_rs.at[1], next1)

    def t_copy(c):
        part = pl.ds(c * CHUNK, CHUNK)
        return remote(tt.at[part], tlow.at[part], t_ss.at[c], t_rs.at[c], next1)

    @pl.when(low)
    def _():
        dt_copy().start()

    for c in range(CHUNKS):
        sl = slice(c * CHUNK, c * CHUNK + CHUNK)
        if c % (CHUNKS // 2) == 0:
            l_copy(c // (CHUNKS // 2)).wait_recv()
        tt[sl, :] = doth8[0:1, :] * lme[sl, :] + lother[sl, :]

        @pl.when(low)
        def _():
            t_copy(c).start()

    @pl.when(low)
    def _():
        tlow[...] = jnp.zeros((STATE, WIDTH), F32)
        dlow8[...] = jnp.ones((8, WIDTH), F32)

    @pl.when(opens)
    def _():
        xin[...] = jnp.zeros((STATE, WIDTH), F32)

    def x_copy(c, far):
        part = pl.ds(c * CHUNK, CHUNK)
        if far:
            return remote(xsend.at[part], xin.at[part], x2_ss.at[c], x_rs.at[c], next2)
        return remote(xnsend.at[part], xnear.at[part], x_ss.at[c], n_rs.at[c], next1)

    def e_copy(c):
        part = pl.ds(c * CHUNK, CHUNK)
        return remote(epart.at[part], ebuf.at[core, part], e_ss.at[c], e_rs.at[c], other_core)

    def chain():
        @pl.when(high)
        def _():
            dt_copy().wait_recv()

        a = dlow8[0:1, :]
        dchip = dchip8[0:1, :]
        dd = dchip * a
        dm = dme8[0:1, :]
        def forward_chunk(c):
            sl = slice(c * CHUNK, c * CHUNK + CHUNK)

            @pl.when(high)
            def _():
                t_copy(c).wait_recv()

            @pl.when(jnp.logical_and(high, jnp.logical_not(opens)))
            def _():
                x_copy(c, True).wait_recv()

            @pl.when(jnp.logical_and(low, jnp.logical_not(opens)))
            def _():
                x_copy(c, False).wait_recv()
                xin[sl, :] = xnear[sl, :].astype(F32)

            @pl.when(sends_on)
            def _():
                xsend[sl, :] = dd * xin[sl, :] + (dchip * tlow[sl, :] + tt[sl, :])
                x_copy(c, True).start()
                xnsend[sl, :] = xsend[sl, :].astype(BF16)

        def use_chunk(c):
            sl = slice(c * CHUNK, c * CHUNK + CHUNK)
            em = a * xin[sl, :] + tlow[sl, :]
            ebuf[core, sl, :] = em
            epart[sl, :] = dm * em + lme[sl, :]
            e_copy(c).start()

        for c in range(CHUNKS + NEAR_LAG):
            if c < CHUNKS:
                forward_chunk(c)
            if c >= NEAR_LAG:
                pl.when(sends_on)(x_copy(c - NEAR_LAG, False).start)
            if 1 <= c <= CHUNKS:
                use_chunk(c - 1)

    def inside():
        scores = dot_t(k_ref[...], q_ref[...]) + dot_t(kp[...], qp[...])
        causal = rows <= cols
        left = iota((LEN, LEN), 1) < 64
        col_s[...] = jnp.zeros((LEN, LEN), F32)
        weights = jnp.zeros((LEN, LEN), F32)
        for j in range(HEADS // 2):
            lanes = slice(j * 128, j * 128 + 128)
            ogb = og_ref[:, lanes]
            vh, vl = vhi[:, lanes], vlo[:, lanes]
            none = jnp.zeros_like(vh)
            halves = []
            for e in range(2):
                h = 2 * j + e
                own = left if e == 0 else jnp.logical_not(left)
                pd = dot_t(jnp.where(own, vh, none), ogb) + dot_t(jnp.where(own, vl, none), ogb)
                gap = cum_t[h : h + 1, :] - columns[:, h : h + 1]
                dm = jnp.exp(jnp.where(causal, gap, -1e30))
                st = columns[:, 8 + h : 9 + h]
                dm_st = dm * st
                weights = weights + dm_st * pd
                eff = dm * scores * pd
                col_s[:, h : h + 1] = jnp.sum(eff, axis=1, keepdims=True)
                row_s[h : h + 1, :] = jnp.sum(eff * st, axis=0, keepdims=True)
                halves.append(dot((dm_st * scores).astype(BF16), ogb))
            within[:, lanes] = jnp.where(left, halves[0], halves[1])
        w16 = weights.astype(BF16)
        w16_t = weights.T.astype(BF16)
        k_far[...] = dot(w16, qp[...])
        q_far[...] = dot(w16_t, kp[...])
        k_in[...] = dot(w16, q_ref[...])
        q_in[...] = dot(w16_t, k_ref[...])
        skips = jnp.broadcast_to(skip_ref[...], (LEN, HEADS))
        sk_hi, sk_lo = split2(skips)
        skip_row = (dot(sk_hi, heads_rows) + dot(sk_lo, heads_rows))[0:1, :]
        within[...] = within[...] + skip_row * og_ref[...].astype(F32)

    k_back = remote(kpart, krecv, f_ss.at[0], f_rs.at[0], partner)
    q_back = remote(qpart, qrecv, f_ss.at[1], f_rs.at[1], partner)
    c_copy = remote(ext.at[pl.ds(0, 8)], ext.at[pl.ds(LEN, 8)], c_ss.at[0], c_rs.at[0], before)

    def both(a, b):
        return dot(a, b[0]) + dot(a, b[1])

    def with_entering():
        @pl.when(core == 1)
        def _():
            for c in range(CHUNKS):
                e_copy(c).wait_recv()

        far = split2(ebuf[0, HALF:, :])
        qpart[...] = (q_far[...] + dot_t(shi[...], far[0])).astype(BF16)
        q_back.start()
        own = split2(ebuf[0, 0:HALF, :])
        out_of = both(q_ref[...], own) + both(qp[...], far)
        read_s[...] = by_head(og_ref[...].astype(F32) * out_of)
        q_in[...] = q_in[...] + dot_t(shi[...], own[0])

    def with_arriving():
        @pl.when(core == 0)
        def _():
            for c in range(CHUNKS):
                e_copy(c).wait_recv()

        far = split2(ebuf[1, HALF:, :])
        kpart[...] = (k_far[...] + dot_t(whi[...], far[0])).astype(BF16)
        k_back.start()
        own = split2(ebuf[1, 0:HALF, :])
        into = both(k_ref[...], own) + both(kp[...], far)
        ext[0:LEN, :] = (within[...] + tsx[...] * into) * dsilu[...]

        @pl.when(seq > 0)
        def _():
            c_copy.start()

        carried_s[...] = by_head(vals[...] * into)
        k_in[...] = k_in[...] + dot_t(whi[...], own[0])

    mine = jnp.where(forward, 2, 3)
    theirs = 5 - mine

    def turn(i, carry):
        early = jnp.where(i < 2, jnp.where(jnp.logical_xor(i == 0, opens), 1, 0), jnp.where(i == 2, mine, theirs))
        later = jnp.where(i == 0, 1, jnp.where(i == 1, theirs, jnp.where(i == 2, 0, mine)))
        what = jnp.where(late, later, early)
        for n, part in enumerate((chain, inside, with_entering, with_arriving)):
            pl.when(what == n)(part)
        return carry

    lax.fori_loop(0, 4, turn, 0)

    @pl.when(seq == n_seq - 1)
    def _():
        ext[LEN : LEN + 8, :] = jnp.zeros((8, WIDTH), F32)

    cross = jnp.sum(ebuf[0] * ebuf[1], axis=0, keepdims=True)
    cross = by_head(jnp.broadcast_to(cross, (8, WIDTH)))[:, 0:1]
    col = col_s[...].T[0:HEADS, :]
    carried = carried_s[...]
    sgrad_ref[...] = col + to_end * carried
    lh, ll = split2(row_s[...] - col * step_t + from_start * read_s[...])
    eh, el = split2(to_end * step_t * carried)
    since = flag(rows >= cols)
    strict = flag(rows < cols)
    decay = dot(lh, since) + dot(ll, since) + dot(eh, strict) + dot(el, strict)
    dgrad_ref[...] = decay + jnp.exp(total) * cross

    @pl.when(seq < n_seq - 1)
    def _():
        c_copy.wait_recv()

    acc = cw_ref[3:4, :] * ext[0:LEN, :]
    for tap in range(3):
        acc = acc + cw_ref[tap : tap + 1, :] * ext[3 - tap : 3 - tap + LEN, :]
    igrad_ref[...] = acc.astype(BF16)

    k_back.wait_recv()
    kgrad_ref[...] = k_in[...] + krecv[...].astype(F32)
    q_back.wait_recv()
    qgrad_ref[...] = q_in[...] + qrecv[...].astype(F32)

    k_copy.wait_send()
    q_copy.wait_send()
    d_copy.wait_send()
    for half in range(2):
        l_copy(half).wait_send()

    @pl.when(low)
    def _():
        dt_copy().wait_send()
        for c in range(CHUNKS):
            t_copy(c).wait_send()

    @pl.when(sends_on)
    def _():
        for c in range(CHUNKS):
            x_copy(c, True).wait_send()
            x_copy(c, False).wait_send()

    for c in range(CHUNKS):
        e_copy(c).wait_send()
    k_back.wait_send()
    q_back.wait_send()

    @pl.when(seq > 0)
    def _():
        c_copy.wait_send()


def store_kernel(*refs):
    sems = refs[-1]
    moves = [pltpu.make_async_copy(refs[n], refs[n + 5], sems.at[n]) for n in range(5)]
    for move in moves:
        move.start()
    for move in moves:
        move.wait()


def body(n_seq, conv_output, output_grad, write_keys, read_queries, log_decay, step_size, skip_gain, conv_weight):
    shape = jax.ShapeDtypeStruct
    vmem = pltpu.VMEM
    dma = pltpu.SemaphoreType.DMA
    big = (STATE, WIDTH)
    tok = (LEN, WIDTH)
    sq = (LEN, LEN)
    small = (HEADS, LEN)
    row = (8, WIDTH)
    in_vmem = pl.BlockSpec(memory_space=vmem)
    hbm = pl.BlockSpec(memory_space=pltpu.HBM)
    outs = (shape(tok, BF16), shape(sq, F32), shape(sq, F32), shape(small, F32), shape(small, F32))
    results = pl.pallas_call(
        functools.partial(kernel, n_seq),
        out_shape=tuple(vmem(o.shape, o.dtype) for o in outs),
        in_specs=[hbm] * 8,
        out_specs=(in_vmem,) * 5,
        scratch_shapes=[
            vmem(tok, BF16), vmem(tok, BF16), vmem(sq, BF16), vmem(sq, BF16),
            vmem(small, F32), vmem(small, F32), vmem((1, HEADS), F32), vmem((4, WIDTH), F32),
            vmem(sq, F32), vmem(sq, F32), vmem(small, F32), vmem(sq, BF16), vmem(sq, BF16),
            vmem(tok, BF16), vmem(tok, BF16), vmem(tok, F32), vmem(tok, F32), vmem(tok, F32),
            vmem(tok, BF16), vmem(tok, BF16), vmem(tok, BF16), vmem(tok, BF16), vmem(tok, F32),
            vmem(sq, F32), vmem(sq, F32), vmem(sq, F32), vmem(sq, F32), vmem(small, F32), vmem(small, F32),
            vmem(big, F32), vmem(big, F32), vmem(big, F32),
            vmem(big, F32), vmem(big, F32),
            vmem(row, F32), vmem(row, F32), vmem(row, F32), vmem(row, F32),
            vmem(big, F32), vmem(big, F32), vmem(big, BF16), vmem(big, BF16), vmem((2,) + big, F32), vmem(big, F32),
            vmem((LEN + 8, WIDTH), F32), vmem(sq, BF16), vmem(sq, BF16), vmem(sq, BF16), vmem(sq, BF16),
            dma((8,)), dma((2,)), dma((2,)), dma((2,)), dma((2,)), dma((2,)), dma((2,)),
            dma((CHUNKS,)), dma((CHUNKS,)),
            dma((CHUNKS,)), dma((CHUNKS,)), dma((CHUNKS,)), dma((CHUNKS,)), dma((CHUNKS,)), dma((CHUNKS,)),
            dma((2,)), dma((2,)), dma((1,)), dma((1,)),
        ],
        compiler_params=pltpu.CompilerParams(
            collective_id=0, has_side_effects=True, vmem_limit_bytes=VMEM_BYTES
        ),
        cost_estimate=pl.CostEstimate(flops=300_000_000, bytes_accessed=1_000_000, transcendentals=300_000),
    )(
        conv_output, output_grad, write_keys, read_queries, log_decay.T, step_size.T,
        skip_gain.reshape(1, HEADS), conv_weight,
    )
    igrad, kgrad, qgrad, dgrad, sgrad = pl.pallas_call(
        store_kernel,
        out_shape=outs,
        in_specs=[pl.BlockSpec(memory_space=pl.ANY)] * 5,
        out_specs=(hbm,) * 5,
        scratch_shapes=[dma((5,))],
        compiler_params=pltpu.CompilerParams(vmem_limit_bytes=16 * 1024 * 1024),
    )(*results)
    return igrad, kgrad, qgrad, dgrad.T, sgrad.T


def solution(mesh):
    spec = P("seq", "head")
    return jax.shard_map(
        functools.partial(body, mesh.shape["seq"]),
        mesh=mesh,
        in_specs=(spec, spec, spec, spec, spec, spec, P("head"), P(None, "head")),
        out_specs=(spec,) * 5,
        check_vma=False,
    )
```

```python
import functools

import jax
import jax.numpy as jnp
from jax import lax
from jax.experimental import pallas as pl
from jax.experimental.pallas import tpu as pltpu
from jax.sharding import PartitionSpec as P

MESH = pl.DeviceIdType.MESH
F32 = jnp.float32
BF16 = jnp.bfloat16
LEN = 128
WIDTH = 512
HEADS = 8
HALF = 128
VMEM_BYTES = 58000 * 1024
STATE = 256
CHUNK = 16
CHUNKS = STATE // CHUNK
NEAR_LAG = 6


def dot(a, b):
    return lax.dot_general(a, b, (((1,), (0,)), ((), ())), preferred_element_type=F32)


def dot_t(a, b):
    return lax.dot_general(a, b, (((1,), (1,)), ((), ())), preferred_element_type=F32)


def split2(x):
    hi = x.astype(BF16)
    return hi, (x - hi.astype(F32)).astype(BF16)


def split3(x):
    hi = x.astype(BF16)
    rest = x - hi.astype(F32)
    mid = rest.astype(BF16)
    return hi, mid, (rest - mid.astype(F32)).astype(BF16)


def iota(shape, axis):
    return lax.broadcasted_iota(jnp.int32, shape, axis)


def flag(cond):
    return cond.astype(F32).astype(BF16)


def kernel(
    n_seq, conv_hbm, og_hbm, k_hbm, q_hbm, ld_hbm, ss_hbm, skip_hbm, cw_hbm,
    igrad_ref, kgrad_ref, qgrad_ref, dgrad_ref, sgrad_ref,
    conv_ref, og_ref, k_ref, q_ref, ld_ref, ss_ref, skip_ref, cw_ref,
    pack, col_s, row_s, kp, qp, vhi, vlo, vals, dsilu, tsx, whi, wlo, shi, slo, within,
    k_in, q_in, k_far, q_far, read_s, carried_s, out_acc, into_acc,
    lme, lsend, lother, tt, tlow, dme8, doth8, dchip8, dlow8, xin, xsend, xnear, xnsend, ebuf, epart,
    ext, kpart, qpart, krecv, qrecv, alpha, beta, alpha_r, beta_r, crow, k_top, kp_top,
    in_s, kq_ss, kq_rs, d_ss, d_rs, l_ss, l_rs, t_ss, t_rs, x_ss, x2_ss, x_rs, n_rs, e_ss, e_rs, f_ss, f_rs, c_ss, c_rs, a_ss, a_rs,
):
    seq = lax.axis_index("seq")
    head = lax.axis_index("head")
    core = lax.rem(seq, 2)
    chip = seq // 2
    chips = n_seq // 2
    pos = jnp.where(core == 0, chip, chips - 1 - chip)
    group = pos // 2
    high = lax.rem(pos, 2) == 1
    low = lax.rem(pos, 2) == 0
    opens = group == 0
    late = group >= 3 * chips // 8
    middle = group >= chips // 4
    last_group = chips // 2 - 1
    closes = group == last_group
    sends_on = jnp.logical_and(high, group < last_group)
    sends_last = jnp.logical_and(high, group == last_group - 1)
    sends_far = jnp.logical_and(high, group < last_group - 1)
    inner = jnp.logical_not(opens)
    takes32 = jnp.logical_and(inner, jnp.logical_and(high, jnp.logical_not(closes)))
    takes16 = jnp.logical_and(inner, jnp.logical_or(low, closes))
    step1 = jnp.where(core == 0, 2, n_seq - 2)
    step2 = jnp.where(core == 0, 4, n_seq - 4)

    def at(s):
        return (lax.rem(s, n_seq), head)

    next1 = at(seq + step1)
    next2 = at(seq + step2)
    other_core = at(seq + 1 - 2 * core)
    partner = (seq, head + 1 - 2 * lax.rem(head, 2))

    barrier = pltpu.get_barrier_semaphore()
    greeted = (
        at(seq + 2), at(seq + n_seq - 2), at(seq + 4), at(seq + n_seq - 4), other_core, partner,
    )
    for peer in greeted:
        pl.semaphore_signal(barrier, inc=1, device_id=peer, device_id_type=MESH)

    moves = [
        pltpu.make_async_copy(src, dst, in_s.at[n])
        for n, (src, dst) in enumerate((
            (ld_hbm, ld_ref), (ss_hbm, ss_ref), (conv_hbm, conv_ref), (og_hbm, og_ref),
            (k_hbm, k_ref), (q_hbm, q_ref), (skip_hbm, skip_ref), (cw_hbm, cw_ref),
        ))
    ]
    for move in moves:
        move.start()

    def remote(src, dst, ss, rs, peer):
        return pltpu.make_async_remote_copy(
            src_ref=src, dst_ref=dst, send_sem=ss, recv_sem=rs, device_id=peer, device_id_type=MESH
        )

    pl.semaphore_wait(barrier, len(greeted))
    k_copy = remote(k_hbm, kp, kq_ss.at[0], kq_rs.at[0], partner)
    q_copy = remote(q_hbm, qp, kq_ss.at[1], kq_rs.at[1], partner)
    k_copy.start()
    q_copy.start()

    rows = iota((LEN, LEN), 0)
    cols = iota((LEN, LEN), 1)
    upto = flag(rows <= cols)
    pack[...] = jnp.zeros((LEN, LEN), F32)
    heads_rows = flag(iota((HEADS, WIDTH), 0) == iota((HEADS, WIDTH), 1) // 64)

    def spread(base):
        return flag(iota((LEN, WIDTH), 0) - base == iota((LEN, WIDTH), 1) // 64)

    def by_head(x):
        hi, lo = split2(x)
        return dot_t(heads_rows, hi) + dot_t(heads_rows, lo)

    moves[0].wait()
    moves[1].wait()
    hi, mid, lo = split3(ld_ref[...])
    cum_t = dot(hi, upto) + (dot(mid, upto) + dot(lo, upto))
    step_t = ss_ref[...]
    total = cum_t[:, LEN - 1 : LEN]
    from_start = jnp.exp(cum_t)
    to_end = jnp.exp(total - cum_t)
    pack[0:8, :] = cum_t
    pack[8:16, :] = step_t
    pack[16:24, :] = from_start
    pack[24:32, :] = to_end * step_t
    columns = pack[...].T
    c_hi, c_lo = split2(columns)
    fs_sel, ts_sel = spread(16), spread(24)
    fsx = dot(c_hi, fs_sel) + dot(c_lo, fs_sel)
    tsx[...] = dot(c_hi, ts_sel) + dot(c_lo, ts_sel)
    dme8[...] = jnp.broadcast_to(fsx[LEN - 1 : LEN, :], (8, WIDTH))

    d_copy = remote(dme8, doth8, d_ss.at[0], d_rs.at[0], other_core)
    d_copy.start()

    moves[2].wait()
    preact = conv_ref[...].astype(F32)
    sig = 1.0 / (1.0 + jnp.exp(-preact))
    value = preact * sig
    vals[...] = value
    vhi[...], vlo[...] = split2(value)
    dsilu[...] = sig * (1.0 + preact * (1.0 - sig))
    whi[...], wlo[...] = split2(value * tsx[...])
    moves[3].wait()
    shi[...], slo[...] = split2(og_ref[...].astype(F32) * fsx)

    forward = core == 0

    def turned(x):
        return x.astype(F32).T.astype(BF16)

    def l_copy(half):
        part = pl.ds(half * HALF, HALF)
        return remote(lsend.at[part], lother.at[part], l_ss.at[half], l_rs.at[half], other_core)

    def local_half(half, kk, qq):
        sl = slice(half * HALF, half * HALF + HALF)
        kt, qt = turned(kk), turned(qq)
        wh, wl, sh, slw = whi[...], wlo[...], shi[...], slo[...]
        mine, other = jnp.where(forward, kt, qt), jnp.where(forward, qt, kt)
        lsend[sl, :] = dot(other, jnp.where(forward, sh, wh)) + dot(other, jnp.where(forward, slw, wl))
        l_copy(half).start()
        lme[sl, :] = dot(mine, jnp.where(forward, wh, sh)) + dot(mine, jnp.where(forward, wl, slw))

    moves[4].wait()
    moves[5].wait()
    k_copy.wait_recv()
    q_copy.wait_recv()
    local_half(1, kp[...], qp[...])
    local_half(0, k_ref[...], q_ref[...])
    moves[6].wait()
    moves[7].wait()

    d_copy.wait_recv()
    dchip8[...] = dme8[...] * doth8[...]

    def first_row(c):
        return (c * CHUNK + HALF) % STATE

    def dt_copy():
        return remote(dchip8, dlow8, d_ss.at[1], d_rs.at[1], next1)

    def t_copy(c):
        part = pl.ds(first_row(c), CHUNK)
        return remote(tt.at[part], tlow.at[part], t_ss.at[c], t_rs.at[c], next1)

    @pl.when(low)
    def _():
        dt_copy().start()

    for c in range(CHUNKS):
        sl = slice(first_row(c), first_row(c) + CHUNK)
        if c % (CHUNKS // 2) == 0:
            l_copy(1 - c // (CHUNKS // 2)).wait_recv()
        tt[sl, :] = doth8[0:1, :] * lme[sl, :] + lother[sl, :]

        @pl.when(low)
        def _():
            t_copy(c).start()

    @pl.when(low)
    def _():
        tlow[...] = jnp.zeros((STATE, WIDTH), F32)
        dlow8[...] = jnp.ones((8, WIDTH), F32)

    @pl.when(opens)
    def _():
        xin[...] = jnp.zeros((STATE, WIDTH), F32)

    def x_copy(c):
        part = pl.ds(first_row(c), CHUNK)
        return remote(xsend.at[part], xin.at[part], x2_ss.at[c], x_rs.at[c], next2)

    def leaf_copy(c):
        part = pl.ds(first_row(c), CHUNK)
        return remote(xnsend.at[part], xnear.at[part], x_ss.at[c], n_rs.at[c], next1)

    def last_copy(c):
        part = pl.ds(first_row(c), CHUNK)
        return remote(xnsend.at[part], xnear.at[part], x2_ss.at[c], n_rs.at[c], next2)

    def e_copy(c):
        part = pl.ds(first_row(c), CHUNK)
        return remote(epart.at[part], ebuf.at[core, part], e_ss.at[c], e_rs.at[c], other_core)

    def chain(half):
        if half == 0:

            @pl.when(high)
            def _():
                dt_copy().wait_recv()

        a = dlow8[0:1, :]
        dchip = dchip8[0:1, :]
        dd = dchip * a
        dm = dme8[0:1, :]

        def forward_chunk(c):
            sl = slice(first_row(c), first_row(c) + CHUNK)

            @pl.when(high)
            def _():
                t_copy(c).wait_recv()

            @pl.when(takes32)
            def _():
                x_copy(c).wait_recv()

            @pl.when(takes16)
            def _():
                leaf_copy(c).wait_recv()
                xin[sl, :] = xnear[sl, :].astype(F32)

            @pl.when(sends_far)
            def _():
                x = dd * xin[sl, :] + (dchip * tlow[sl, :] + tt[sl, :])
                xsend[sl, :] = x
                x_copy(c).start()
                xnsend[sl, :] = x.astype(BF16)

            @pl.when(sends_last)
            def _():
                x = dd * xin[sl, :] + (dchip * tlow[sl, :] + tt[sl, :])
                xnsend[sl, :] = x.astype(BF16)
                last_copy(c).start()
                leaf_copy(c).start()

        def use_chunk(c):
            sl = slice(first_row(c), first_row(c) + CHUNK)
            em = a * xin[sl, :] + tlow[sl, :]
            ebuf[core, sl, :] = em
            epart[sl, :] = dm * em + lme[sl, :]
            e_copy(c).start()

        start, stop = (0, CHUNKS // 2) if half == 0 else (CHUNKS // 2, CHUNKS)
        for c in range(start, stop):
            forward_chunk(c)
            if c >= NEAR_LAG:
                pl.when(sends_far)(leaf_copy(c - NEAR_LAG).start)
            if c > start:
                use_chunk(c - 1)
        if half == 1:

            @pl.when(sends_far)
            def _():
                for c in range(CHUNKS - NEAR_LAG, CHUNKS):
                    leaf_copy(c).start()

        use_chunk(stop - 1)

    ahead = [
        remote(src, dst, a_ss.at[n], a_rs.at[n], other_core)
        for n, (src, dst) in enumerate((
            (alpha, alpha_r), (beta, beta_r), (k_ref.at[pl.ds(0, 16)], k_top), (kp.at[pl.ds(0, 16)], kp_top),
        ))
    ]

    def inside():
        scores = dot_t(k_ref[...], q_ref[...]) + dot_t(kp[...], qp[...])
        causal = rows <= cols
        left = iota((LEN, LEN), 1) < 64
        col_s[...] = jnp.zeros((LEN, LEN), F32)
        weights = jnp.zeros((LEN, LEN), F32)
        for j in range(HEADS // 2):
            lanes = slice(j * 128, j * 128 + 128)
            ogb = og_ref[:, lanes]
            vh, vl = vhi[:, lanes], vlo[:, lanes]
            none = jnp.zeros_like(vh)
            halves = []
            for e in range(2):
                h = 2 * j + e
                own = left if e == 0 else jnp.logical_not(left)
                pd = dot_t(jnp.where(own, vh, none), ogb) + dot_t(jnp.where(own, vl, none), ogb)
                gap = cum_t[h : h + 1, :] - columns[:, h : h + 1]
                dm = jnp.exp(jnp.where(causal, gap, -1e30))
                st = columns[:, 8 + h : 9 + h]
                dm_st = dm * st
                weights = weights + dm_st * pd
                eff = dm * scores * pd
                col_s[:, h : h + 1] = jnp.sum(eff, axis=1, keepdims=True)
                row_s[h : h + 1, :] = jnp.sum(eff * st, axis=0, keepdims=True)
                halves.append(dot((dm_st * scores).astype(BF16), ogb))
            within[:, lanes] = jnp.where(left, halves[0], halves[1])
        w16 = weights.astype(BF16)
        w16_t = weights.T.astype(BF16)
        k_far[...] = dot(w16, qp[...])
        q_far[...] = dot(w16_t, kp[...])
        k_in[...] = dot(w16, q_ref[...])
        q_in[...] = dot(w16_t, k_ref[...])
        skips = jnp.broadcast_to(skip_ref[...], (LEN, HEADS))
        sk_hi, sk_lo = split2(skips)
        skip_row = (dot(sk_hi, heads_rows) + dot(sk_lo, heads_rows))[0:1, :]
        within[...] = within[...] + skip_row * og_ref[...].astype(F32)
        alpha[...] = within[0:8, :] * dsilu[0:8, :]
        beta[...] = tsx[0:8, :] * dsilu[0:8, :]

        @pl.when(core == 0)
        def _():
            for move in ahead:
                move.start()

    k_back = remote(kpart, krecv, f_ss.at[0], f_rs.at[0], partner)
    q_back = remote(qpart, qrecv, f_ss.at[1], f_rs.at[1], partner)
    c_far = remote(crow, ext.at[pl.ds(LEN, 8)], c_ss.at[0], c_rs.at[0], next1)
    c_near = remote(ext.at[pl.ds(0, 8)], ext.at[pl.ds(LEN, 8)], c_ss.at[1], c_rs.at[1], other_core)
    sends_rows = jnp.logical_and(core == 1, chip > 0)
    takes_rows = jnp.logical_and(core == 1, chip < chips - 1)

    def both(a, b):
        return dot(a, b[0]) + dot(a, b[1])

    def their_chunks(of_core, half):
        @pl.when(core == of_core)
        def _():
            for c in range(half * (CHUNKS // 2), (half + 1) * (CHUNKS // 2)):
                e_copy(c).wait_recv()

    def entering_far():
        their_chunks(1, 0)
        far = split2(ebuf[0, HALF:, :])
        qpart[...] = (q_far[...] + dot_t(shi[...], far[0])).astype(BF16)
        q_back.start()
        out_acc[...] = both(qp[...], far)

    def entering_own():
        their_chunks(1, 1)
        own = split2(ebuf[0, 0:HALF, :])
        out_of = out_acc[...] + both(q_ref[...], own)
        read_s[...] = by_head(og_ref[...].astype(F32) * out_of)
        q_in[...] = q_in[...] + dot_t(shi[...], own[0])

    def arriving_far():
        their_chunks(0, 0)
        far = split2(ebuf[1, HALF:, :])
        kpart[...] = (k_far[...] + dot_t(whi[...], far[0])).astype(BF16)
        k_back.start()
        into_acc[...] = both(kp[...], far)

    def arriving_own():
        their_chunks(0, 1)
        own = split2(ebuf[1, 0:HALF, :])

        @pl.when(core == 1)
        def _():
            for move in ahead:
                move.wait_recv()
            rows_of = both(k_top[...], split2(epart[0:HALF, :])) + both(kp_top[...], split2(epart[HALF:, :]))
            crow[...] = alpha_r[...] + beta_r[...] * rows_of[0:8, :]
            pl.when(sends_rows)(c_far.start)

        into = into_acc[...] + both(k_ref[...], own)
        ext[0:LEN, :] = (within[...] + tsx[...] * into) * dsilu[...]
        pl.when(core == 1)(c_near.start)
        carried_s[...] = by_head(vals[...] * into)
        k_in[...] = k_in[...] + dot_t(whi[...], own[0])

    parts = (
        inside, functools.partial(chain, 0), functools.partial(chain, 1),
        entering_far, entering_own, arriving_far, arriving_own,
    )
    mine = jnp.where(forward, 3, 5)
    theirs = 8 - mine

    def turn(i, carry):
        def pick(*order):
            what = jnp.int32(0)
            for n, part in enumerate(order):
                what = jnp.where(i == n, part, what)
            return what

        what = jnp.where(
            opens, pick(1, 2, 0, mine, mine + 1, theirs, theirs + 1),
            jnp.where(
                closes, pick(0, theirs, theirs + 1, 1, mine, 2, mine + 1),
                jnp.where(
                    late, pick(0, theirs, theirs + 1, 1, 2, mine, mine + 1),
                    jnp.where(
                        middle, pick(0, 1, 2, theirs, theirs + 1, mine, mine + 1),
                        pick(0, 1, 2, mine, mine + 1, theirs, theirs + 1),
                    ),
                ),
            ),
        )
        for n, part in enumerate(parts):
            pl.when(what == n)(part)
        return carry

    lax.fori_loop(0, len(parts), turn, 0)

    @pl.when(seq == n_seq - 1)
    def _():
        ext[LEN : LEN + 8, :] = jnp.zeros((8, WIDTH), F32)

    cross = jnp.sum(ebuf[0] * ebuf[1], axis=0, keepdims=True)
    cross = by_head(jnp.broadcast_to(cross, (8, WIDTH)))[:, 0:1]
    col = col_s[...].T[0:HEADS, :]
    carried = carried_s[...]
    sgrad_ref[...] = col + to_end * carried
    lh, ll = split2(row_s[...] - col * step_t + from_start * read_s[...])
    eh, el = split2(to_end * step_t * carried)
    since = flag(rows >= cols)
    strict = flag(rows < cols)
    decay = dot(lh, since) + dot(ll, since) + dot(eh, strict) + dot(el, strict)
    dgrad_ref[...] = decay + jnp.exp(total) * cross

    def convolve(first, stop):
        acc = cw_ref[3:4, :] * ext[first:stop, :]
        for tap in range(3):
            acc = acc + cw_ref[tap : tap + 1, :] * ext[first + 3 - tap : stop + 3 - tap, :]
        igrad_ref[first:stop, :] = acc.astype(BF16)

    convolve(0, LEN - 16)

    k_back.wait_recv()
    kgrad_ref[...] = k_in[...] + krecv[...].astype(F32)
    q_back.wait_recv()
    qgrad_ref[...] = q_in[...] + qrecv[...].astype(F32)

    pl.when(core == 0)(c_near.wait_recv)
    pl.when(takes_rows)(c_far.wait_recv)
    convolve(LEN - 16, LEN)

    k_copy.wait_send()
    q_copy.wait_send()
    d_copy.wait_send()
    for half in range(2):
        l_copy(half).wait_send()

    @pl.when(low)
    def _():
        dt_copy().wait_send()
        for c in range(CHUNKS):
            t_copy(c).wait_send()

    @pl.when(sends_on)
    def _():
        for c in range(CHUNKS):
            leaf_copy(c).wait_send()

    @pl.when(sends_far)
    def _():
        for c in range(CHUNKS):
            x_copy(c).wait_send()

    @pl.when(sends_last)
    def _():
        for c in range(CHUNKS):
            last_copy(c).wait_send()

    for c in range(CHUNKS):
        e_copy(c).wait_send()
    k_back.wait_send()
    q_back.wait_send()

    @pl.when(core == 0)
    def _():
        for move in ahead:
            move.wait_send()

    pl.when(core == 1)(c_near.wait_send)
    pl.when(sends_rows)(c_far.wait_send)


def store_kernel(*refs):
    sems = refs[-1]
    moves = [pltpu.make_async_copy(refs[n], refs[n + 5], sems.at[n]) for n in range(5)]
    for move in moves:
        move.start()
    for move in moves:
        move.wait()


def body(n_seq, conv_output, output_grad, write_keys, read_queries, log_decay, step_size, skip_gain, conv_weight):
    shape = jax.ShapeDtypeStruct
    vmem = pltpu.VMEM
    dma = pltpu.SemaphoreType.DMA
    big = (STATE, WIDTH)
    tok = (LEN, WIDTH)
    sq = (LEN, LEN)
    small = (HEADS, LEN)
    row = (8, WIDTH)
    in_vmem = pl.BlockSpec(memory_space=vmem)
    hbm = pl.BlockSpec(memory_space=pltpu.HBM)
    outs = (shape(tok, BF16), shape(sq, F32), shape(sq, F32), shape(small, F32), shape(small, F32))
    results = pl.pallas_call(
        functools.partial(kernel, n_seq),
        out_shape=tuple(vmem(o.shape, o.dtype) for o in outs),
        in_specs=[hbm] * 8,
        out_specs=(in_vmem,) * 5,
        scratch_shapes=[
            vmem(tok, BF16), vmem(tok, BF16), vmem(sq, BF16), vmem(sq, BF16),
            vmem(small, F32), vmem(small, F32), vmem((1, HEADS), F32), vmem((4, WIDTH), F32),
            vmem(sq, F32), vmem(sq, F32), vmem(small, F32), vmem(sq, BF16), vmem(sq, BF16),
            vmem(tok, BF16), vmem(tok, BF16), vmem(tok, F32), vmem(tok, F32), vmem(tok, F32),
            vmem(tok, BF16), vmem(tok, BF16), vmem(tok, BF16), vmem(tok, BF16), vmem(tok, F32),
            vmem(sq, F32), vmem(sq, F32), vmem(sq, F32), vmem(sq, F32), vmem(small, F32), vmem(small, F32),
            vmem(tok, F32), vmem(tok, F32),
            vmem(big, F32), vmem(big, F32), vmem(big, F32),
            vmem(big, F32), vmem(big, F32),
            vmem(row, F32), vmem(row, F32), vmem(row, F32), vmem(row, F32),
            vmem(big, F32), vmem(big, F32), vmem(big, BF16), vmem(big, BF16), vmem((2,) + big, F32), vmem(big, F32),
            vmem((LEN + 8, WIDTH), F32), vmem(sq, BF16), vmem(sq, BF16), vmem(sq, BF16), vmem(sq, BF16),
            vmem(row, F32), vmem(row, F32), vmem(row, F32), vmem(row, F32), vmem(row, F32),
            vmem((16, LEN), BF16), vmem((16, LEN), BF16),
            dma((8,)), dma((2,)), dma((2,)), dma((2,)), dma((2,)), dma((2,)), dma((2,)),
            dma((CHUNKS,)), dma((CHUNKS,)),
            dma((CHUNKS,)), dma((CHUNKS,)), dma((CHUNKS,)), dma((CHUNKS,)), dma((CHUNKS,)), dma((CHUNKS,)),
            dma((2,)), dma((2,)), dma((2,)), dma((2,)), dma((4,)), dma((4,)),
        ],
        compiler_params=pltpu.CompilerParams(
            collective_id=0, has_side_effects=True, vmem_limit_bytes=VMEM_BYTES
        ),
        cost_estimate=pl.CostEstimate(flops=300_000_000, bytes_accessed=1_000_000, transcendentals=300_000),
    )(
        conv_output, output_grad, write_keys, read_queries, log_decay.T, step_size.T,
        skip_gain.reshape(1, HEADS), conv_weight,
    )
    igrad, kgrad, qgrad, dgrad, sgrad = pl.pallas_call(
        store_kernel,
        out_shape=outs,
        in_specs=[pl.BlockSpec(memory_space=pl.ANY)] * 5,
        out_specs=(hbm,) * 5,
        scratch_shapes=[dma((5,))],
        compiler_params=pltpu.CompilerParams(vmem_limit_bytes=16 * 1024 * 1024),
    )(*results)
    return igrad, kgrad, qgrad, dgrad.T, sgrad.T


def solution(mesh):
    spec = P("seq", "head")
    return jax.shard_map(
        functools.partial(body, mesh.shape["seq"]),
        mesh=mesh,
        in_specs=(spec, spec, spec, spec, spec, spec, P("head"), P(None, "head")),
        out_specs=(spec,) * 5,
        check_vma=False,
    )
```

```python
import functools

import jax
import jax.numpy as jnp
from jax import lax
from jax.experimental import pallas as pl
from jax.experimental.pallas import tpu as pltpu
from jax.sharding import PartitionSpec as P

MESH = pl.DeviceIdType.MESH
F32 = jnp.float32
BF16 = jnp.bfloat16
LEN = 128
WIDTH = 512
HEADS = 8
HALF = 128
VMEM_BYTES = 58000 * 1024
STATE = 256
CHUNK = 16
CHUNKS = STATE // CHUNK
NEAR_LAG = 6
PIECE = 4
HEAD_CHUNKS = HALF // 2 // CHUNK
FAR_DONE = CHUNKS - HEAD_CHUNKS


def dot(a, b):
    return lax.dot_general(a, b, (((1,), (0,)), ((), ())), preferred_element_type=F32)


def dot_t(a, b):
    return lax.dot_general(a, b, (((1,), (1,)), ((), ())), preferred_element_type=F32)


def split2(x):
    hi = x.astype(BF16)
    return hi, (x - hi.astype(F32)).astype(BF16)


def split3(x):
    hi = x.astype(BF16)
    rest = x - hi.astype(F32)
    mid = rest.astype(BF16)
    return hi, mid, (rest - mid.astype(F32)).astype(BF16)


def iota(shape, axis):
    return lax.broadcasted_iota(jnp.int32, shape, axis)


def flag(cond):
    return cond.astype(F32).astype(BF16)


def kernel(
    n_seq, conv_hbm, og_hbm, k_hbm, q_hbm, ld_hbm, ss_hbm, skip_hbm, cw_hbm,
    igrad_ref, kgrad_ref, qgrad_ref, dgrad_ref, sgrad_ref,
    conv_ref, og_ref, k_ref, q_ref, ld_ref, ss_ref, skip_ref, cw_ref,
    pack, col_s, row_s, kp, qp, vhi, vlo, vals, dsilu, tsx, whi, wlo, shi, slo, within,
    k_in, q_in, k_far, q_far, read_s, carried_s, out_acc, into_acc,
    lme, lsend, lother, tt, tlow, dme8, doth8, dchip8, dlow8, xin, xsend, xnear, xnsend, ebuf, epart,
    ext, kpart, qpart, krecv, qrecv, alpha, beta, alpha_r, beta_r, crow, crow16, k_top, kp_top, us, ubuf, dgroup8, dbuf, weight,
    in_s, kq_ss, kq_rs, d_ss, d_rs, l_ss, l_rs, t_ss, t_rs, x_ss, x2_ss, x_rs, n_rs, e_ss, e_rs, f_ss, f_rs, c_ss, c_rs, a_ss, a_rs,
    u_ss, u_rs, w_ss, w_rs,
):
    seq = lax.axis_index("seq")
    head = lax.axis_index("head")
    core = lax.rem(seq, 2)
    chip = seq // 2
    chips = n_seq // 2
    pos = jnp.where(core == 0, chip, chips - 1 - chip)
    group = pos // 2
    high = lax.rem(pos, 2) == 1
    low = lax.rem(pos, 2) == 0
    opens = group == 0
    late = group >= 3 * chips // 8
    middle = group >= chips // 4
    groups = chips // 2
    last_group = groups - 1 - core
    closes = group == last_group
    at_end = group == groups - 1
    backward = core == 1
    gathers = jnp.logical_and(backward, jnp.logical_and(high, at_end))
    gives = jnp.logical_and(backward, jnp.logical_and(high, group < groups - 1))
    gives_first = jnp.logical_and(gives, group >= 2)
    sends_on = jnp.logical_and(high, group < last_group)
    sends_last = jnp.logical_and(high, group == last_group - 1)
    sends_far = jnp.logical_and(high, group < last_group - 1)
    inner = jnp.logical_not(opens)
    takes32 = jnp.logical_and(inner, jnp.logical_and(high, jnp.logical_not(jnp.logical_or(closes, gathers))))
    takes16 = jnp.logical_and(inner, jnp.logical_or(low, closes))
    step1 = jnp.where(core == 0, 2, n_seq - 2)
    step2 = jnp.where(core == 0, 4, n_seq - 4)

    def at(s):
        return (lax.rem(s, n_seq), head)

    next1 = at(seq + step1)
    next2 = at(seq + step2)
    other_core = at(seq + 1 - 2 * core)
    partner = (seq, head + 1 - 2 * lax.rem(head, 2))

    barrier = pltpu.get_barrier_semaphore()
    greeted = (
        at(seq + 2), at(seq + n_seq - 2), at(seq + 4), at(seq + n_seq - 4), other_core, partner,
    )
    for peer in greeted:
        pl.semaphore_signal(barrier, inc=1, device_id=peer, device_id_type=MESH)

    moves = [
        pltpu.make_async_copy(src, dst, in_s.at[n])
        for n, (src, dst) in enumerate((
            (ld_hbm, ld_ref), (ss_hbm, ss_ref), (conv_hbm, conv_ref), (og_hbm, og_ref),
            (k_hbm, k_ref), (q_hbm, q_ref), (skip_hbm, skip_ref), (cw_hbm, cw_ref),
        ))
    ]
    for move in moves:
        move.start()

    def remote(src, dst, ss, rs, peer):
        return pltpu.make_async_remote_copy(
            src_ref=src, dst_ref=dst, send_sem=ss, recv_sem=rs, device_id=peer, device_id_type=MESH
        )

    @pl.when(gathers)
    def _():
        for z in range(4, chips - 2, 2):
            pl.semaphore_signal(barrier, inc=1, device_id=(2 * z + 1, head), device_id_type=MESH)

    far_giver = jnp.logical_and(gives, jnp.logical_and(chip >= 4, chip < chips - 2))
    pl.semaphore_wait(barrier, len(greeted) + jnp.where(far_giver, 1, 0))

    k_copy = remote(k_hbm, kp, kq_ss.at[0], kq_rs.at[0], partner)
    q_copy = remote(q_hbm, qp, kq_ss.at[1], kq_rs.at[1], partner)
    k_copy.start()
    q_copy.start()

    rows = iota((LEN, LEN), 0)
    cols = iota((LEN, LEN), 1)
    upto = flag(rows <= cols)
    pack[...] = jnp.zeros((LEN, LEN), F32)
    heads_rows = flag(iota((HEADS, WIDTH), 0) == iota((HEADS, WIDTH), 1) // 64)

    def spread(base):
        return flag(iota((LEN, WIDTH), 0) - base == iota((LEN, WIDTH), 1) // 64)

    def by_head(x):
        hi, lo = split2(x)
        return dot_t(heads_rows, hi) + dot_t(heads_rows, lo)

    moves[0].wait()
    moves[1].wait()
    hi, mid, lo = split3(ld_ref[...])
    cum_t = dot(hi, upto) + (dot(mid, upto) + dot(lo, upto))
    step_t = ss_ref[...]
    total = cum_t[:, LEN - 1 : LEN]
    from_start = jnp.exp(cum_t)
    to_end = jnp.exp(total - cum_t)
    pack[0:8, :] = cum_t
    pack[8:16, :] = step_t
    pack[16:24, :] = from_start
    pack[24:32, :] = to_end * step_t
    columns = pack[...].T
    c_hi, c_lo = split2(columns)
    fs_sel, ts_sel = spread(16), spread(24)
    fsx = dot(c_hi, fs_sel) + dot(c_lo, fs_sel)
    tsx[...] = dot(c_hi, ts_sel) + dot(c_lo, ts_sel)
    dme8[...] = jnp.broadcast_to(fsx[LEN - 1 : LEN, :], (8, WIDTH))

    d_copy = remote(dme8, doth8, d_ss.at[0], d_rs.at[0], other_core)
    d_copy.start()

    moves[2].wait()
    preact = conv_ref[...].astype(F32)
    sig = 1.0 / (1.0 + jnp.exp(-preact))
    value = preact * sig
    vals[...] = value
    vhi[...], vlo[...] = split2(value)
    dsilu[...] = sig * (1.0 + preact * (1.0 - sig))
    whi[...], wlo[...] = split2(value * tsx[...])
    moves[3].wait()
    shi[...], slo[...] = split2(og_ref[...].astype(F32) * fsx)

    forward = core == 0

    def turned(x):
        return x.astype(F32).T.astype(BF16)

    def l_copy(half):
        part = pl.ds(half * HALF, HALF)
        return remote(lsend.at[part], lother.at[part], l_ss.at[half], l_rs.at[half], other_core)

    def local_half(half, kk, qq):
        sl = slice(half * HALF, half * HALF + HALF)
        kt, qt = turned(kk), turned(qq)
        wh, wl, sh, slw = whi[...], wlo[...], shi[...], slo[...]
        mine, other = jnp.where(forward, kt, qt), jnp.where(forward, qt, kt)
        lsend[sl, :] = dot(other, jnp.where(forward, sh, wh)) + dot(other, jnp.where(forward, slw, wl))
        l_copy(half).start()
        lme[sl, :] = dot(mine, jnp.where(forward, wh, sh)) + dot(mine, jnp.where(forward, wl, slw))

    moves[4].wait()
    moves[5].wait()
    local_half(0, k_ref[...], q_ref[...])
    k_copy.wait_recv()
    q_copy.wait_recv()
    local_half(1, kp[...], qp[...])
    moves[6].wait()
    moves[7].wait()

    d_copy.wait_recv()
    dchip8[...] = dme8[...] * doth8[...]

    def first_row(c):
        if c < HEAD_CHUNKS:
            return c * CHUNK
        if c < FAR_DONE:
            return HALF + (c - HEAD_CHUNKS) * CHUNK
        return (c - HALF // CHUNK) * CHUNK

    def dt_copy():
        return remote(dchip8, dlow8, d_ss.at[1], d_rs.at[1], next1)

    def t_copy(c):
        part = pl.ds(first_row(c), CHUNK)
        return remote(tt.at[part], tlow.at[part], t_ss.at[c], t_rs.at[c], next1)

    @pl.when(low)
    def _():
        dt_copy().start()

    for c in range(CHUNKS):
        sl = slice(first_row(c), first_row(c) + CHUNK)
        if c == 0:
            l_copy(0).wait_recv()
        if c == HEAD_CHUNKS:
            l_copy(1).wait_recv()
        tt[sl, :] = doth8[0:1, :] * lme[sl, :] + lother[sl, :]

        @pl.when(low)
        def _():
            t_copy(c).start()

    @pl.when(low)
    def _():
        tlow[...] = jnp.zeros((STATE, WIDTH), F32)
        dlow8[...] = jnp.ones((8, WIDTH), F32)

    @pl.when(opens)
    def _():
        xin[...] = jnp.zeros((STATE, WIDTH), F32)

    def x_copy(c):
        part = pl.ds(first_row(c), CHUNK)
        return remote(xsend.at[part], xin.at[part], x2_ss.at[c], x_rs.at[c], next2)

    def leaf_copy(c):
        part = pl.ds(first_row(c), CHUNK)
        return remote(xnsend.at[part], xnear.at[part], x_ss.at[c], n_rs.at[c], next1)

    def u_copy(g, p):
        part = pl.ds(first_row(p * PIECE), PIECE * CHUNK)
        return remote(us.at[part], ubuf.at[g, part], u_ss.at[p], u_rs.at[g, p], (1, head))

    def w_copy(g):
        return remote(dgroup8, dbuf.at[g], w_ss.at[0], w_rs.at[g], (1, head))

    def back_copy(c):
        part = pl.ds(first_row(c), CHUNK)
        return remote(xnsend.at[part], xnear.at[part], x_ss.at[c], n_rs.at[c], at(seq + 2))

    def give():
        @pl.when(gives)
        def _():
            @pl.when(gives_first)
            def _():
                dt_copy().wait_recv()

            dchip = dchip8[0:1, :]
            dgroup8[...] = dchip8[...] * dlow8[...]
            w_copy(group).start()
            for p in range(CHUNKS // PIECE):
                @pl.when(gives_first)
                def _():
                    for c in range(p * PIECE, p * PIECE + PIECE):
                        t_copy(c).wait_recv()

                sl = slice(first_row(p * PIECE), first_row(p * PIECE) + PIECE * CHUNK)
                us[sl, :] = (dchip * tlow[sl, :] + tt[sl, :]).astype(BF16)
                u_copy(group, p).start()

    def last_copy(c):
        part = pl.ds(first_row(c), CHUNK)
        return remote(xnsend.at[part], xnear.at[part], x2_ss.at[c], n_rs.at[c], next2)

    def e_copy(c):
        part = pl.ds(first_row(c), CHUNK)
        return remote(epart.at[part], ebuf.at[core, part], e_ss.at[c], e_rs.at[c], other_core)

    def chain(half):
        if half == 0:

            @pl.when(jnp.logical_and(high, jnp.logical_not(gives_first)))
            def _():
                dt_copy().wait_recv()

            @pl.when(gathers)
            def _():
                for g in range(groups - 1):
                    w_copy(g).wait_recv()
                share = jnp.ones((1, WIDTH), F32)
                for g in range(groups - 2, -1, -1):
                    weight[g : g + 1, :] = share
                    share = share * dbuf[g, 0:1, :]

        a = dlow8[0:1, :]
        dchip = dchip8[0:1, :]
        dd = dchip * a
        dm = dme8[0:1, :]

        def forward_chunk(c):
            sl = slice(first_row(c), first_row(c) + CHUNK)

            @pl.when(jnp.logical_and(high, jnp.logical_not(gives_first)))
            def _():
                t_copy(c).wait_recv()

            @pl.when(gathers)
            def _():
                if c % PIECE == 0:
                    for g in range(groups - 1):
                        u_copy(g, c // PIECE).wait_recv()
                x = weight[0:1, :] * ubuf[0, sl, :].astype(F32)
                for g in range(1, groups - 1):
                    x = x + weight[g : g + 1, :] * ubuf[g, sl, :].astype(F32)
                xin[sl, :] = x
                xnsend[sl, :] = x.astype(BF16)
                back_copy(c).start()

            @pl.when(takes32)
            def _():
                x_copy(c).wait_recv()

            @pl.when(takes16)
            def _():
                leaf_copy(c).wait_recv()
                xin[sl, :] = xnear[sl, :].astype(F32)

            @pl.when(sends_far)
            def _():
                x = dd * xin[sl, :] + (dchip * tlow[sl, :] + tt[sl, :])
                xsend[sl, :] = x
                x_copy(c).start()
                xnsend[sl, :] = x.astype(BF16)

            @pl.when(sends_last)
            def _():
                x = dd * xin[sl, :] + (dchip * tlow[sl, :] + tt[sl, :])
                xnsend[sl, :] = x.astype(BF16)
                last_copy(c).start()
                leaf_copy(c).start()

        def use_chunk(c):
            sl = slice(first_row(c), first_row(c) + CHUNK)
            em = a * xin[sl, :] + tlow[sl, :]
            ebuf[core, sl, :] = em
            epart[sl, :] = dm * em + lme[sl, :]
            e_copy(c).start()

        start, stop = (0, FAR_DONE) if half == 0 else (FAR_DONE, CHUNKS)
        for c in range(start, stop):
            forward_chunk(c)
            if c >= NEAR_LAG:
                pl.when(sends_far)(leaf_copy(c - NEAR_LAG).start)
            if c > start:
                use_chunk(c - 1)
        if half == 1:

            @pl.when(sends_far)
            def _():
                for c in range(CHUNKS - NEAR_LAG, CHUNKS):
                    leaf_copy(c).start()

        use_chunk(stop - 1)

    ahead = [
        remote(src, dst, a_ss.at[n], a_rs.at[n], other_core)
        for n, (src, dst) in enumerate((
            (alpha, alpha_r), (beta, beta_r), (k_ref.at[pl.ds(0, 16)], k_top), (kp.at[pl.ds(0, 16)], kp_top),
        ))
    ]

    def inside():
        scores = dot_t(k_ref[...], q_ref[...]) + dot_t(kp[...], qp[...])
        causal = rows <= cols
        left = iota((LEN, LEN), 1) < 64
        col_s[...] = jnp.zeros((LEN, LEN), F32)
        weights = jnp.zeros((LEN, LEN), F32)
        for j in range(HEADS // 2):
            lanes = slice(j * 128, j * 128 + 128)
            ogb = og_ref[:, lanes]
            vh, vl = vhi[:, lanes], vlo[:, lanes]
            none = jnp.zeros_like(vh)
            halves = []
            for e in range(2):
                h = 2 * j + e
                own = left if e == 0 else jnp.logical_not(left)
                pd = dot_t(jnp.where(own, vh, none), ogb) + dot_t(jnp.where(own, vl, none), ogb)
                gap = cum_t[h : h + 1, :] - columns[:, h : h + 1]
                dm = jnp.exp(jnp.where(causal, gap, -1e30))
                st = columns[:, 8 + h : 9 + h]
                dm_st = dm * st
                weights = weights + dm_st * pd
                eff = dm * scores * pd
                col_s[:, h : h + 1] = jnp.sum(eff, axis=1, keepdims=True)
                row_s[h : h + 1, :] = jnp.sum(eff * st, axis=0, keepdims=True)
                halves.append(dot((dm_st * scores).astype(BF16), ogb))
            within[:, lanes] = jnp.where(left, halves[0], halves[1])
        w16 = weights.astype(BF16)
        w16_t = weights.T.astype(BF16)
        k_far[...] = dot(w16, qp[...])
        q_far[...] = dot(w16_t, kp[...])
        k_in[...] = dot(w16, q_ref[...])
        q_in[...] = dot(w16_t, k_ref[...])
        skips = jnp.broadcast_to(skip_ref[...], (LEN, HEADS))
        sk_hi, sk_lo = split2(skips)
        skip_row = (dot(sk_hi, heads_rows) + dot(sk_lo, heads_rows))[0:1, :]
        within[...] = within[...] + skip_row * og_ref[...].astype(F32)
        alpha[...] = within[0:8, :] * dsilu[0:8, :]
        beta[...] = tsx[0:8, :] * dsilu[0:8, :]

        @pl.when(core == 0)
        def _():
            for move in ahead:
                move.start()

    k_back = remote(kpart, krecv, f_ss.at[0], f_rs.at[0], partner)
    q_back = remote(qpart, qrecv, f_ss.at[1], f_rs.at[1], partner)
    c_far = remote(crow, ext.at[pl.ds(LEN, 8)], c_ss.at[0], c_rs.at[0], next1)
    c_near = remote(ext.at[pl.ds(0, 8)], ext.at[pl.ds(LEN, 8)], c_ss.at[1], c_rs.at[1], other_core)
    sends_rows = jnp.logical_and(core == 1, chip > 0)
    takes_rows = jnp.logical_and(core == 1, chip < chips - 1)

    def both(a, b):
        return dot(a, b[0]) + dot(a, b[1])

    def their_chunks(of_core, half):
        @pl.when(core == of_core)
        def _():
            for c in range(0, FAR_DONE) if half == 0 else range(FAR_DONE, CHUNKS):
                e_copy(c).wait_recv()

    def entering_far():
        their_chunks(1, 0)
        far = split2(ebuf[0, HALF:, :])
        qpart[...] = (q_far[...] + dot_t(shi[...], far[0])).astype(BF16)
        q_back.start()
        out_acc[...] = both(qp[...], far)

    def entering_own():
        their_chunks(1, 1)
        own = split2(ebuf[0, 0:HALF, :])
        out_of = out_acc[...] + both(q_ref[...], own)
        read_s[...] = by_head(og_ref[...].astype(F32) * out_of)
        q_in[...] = q_in[...] + dot_t(shi[...], own[0])

    def arriving_far():
        their_chunks(0, 0)
        far = split2(ebuf[1, HALF:, :])
        kpart[...] = (k_far[...] + dot_t(whi[...], far[0])).astype(BF16)
        k_back.start()
        into_acc[...] = both(kp[...], far)

        @pl.when(core == 1)
        def _():
            for move in ahead:
                move.wait_recv()
            crow16[...] = both(kp_top[...], split2(epart[HALF:, :]))

    def arriving_own():
        their_chunks(0, 1)
        own = split2(ebuf[1, 0:HALF, :])

        @pl.when(core == 1)
        def _():
            rows_of = both(k_top[...], split2(epart[0:HALF, :])) + crow16[...]
            crow[...] = alpha_r[...] + beta_r[...] * rows_of[0:8, :]
            pl.when(sends_rows)(c_far.start)

        into = into_acc[...] + both(k_ref[...], own)
        ext[0:LEN, :] = (within[...] + tsx[...] * into) * dsilu[...]
        pl.when(core == 1)(c_near.start)
        carried_s[...] = by_head(vals[...] * into)
        k_in[...] = k_in[...] + dot_t(whi[...], own[0])

    parts = (
        inside, functools.partial(chain, 0), functools.partial(chain, 1),
        entering_far, entering_own, arriving_far, arriving_own, give,
    )
    mine = jnp.where(forward, 3, 5)
    theirs = 8 - mine

    def turn(i, carry):
        def pick(*order):
            what = jnp.int32(0)
            for n, part in enumerate(order):
                what = jnp.where(i == n, part, what)
            return what

        what = jnp.where(
            opens, pick(1, 2, 7, 0, mine, mine + 1, theirs, theirs + 1),
            jnp.where(
                jnp.logical_or(closes, at_end), pick(0, 7, theirs, theirs + 1, 1, mine, 2, mine + 1),
                jnp.where(
                    late, pick(0, 7, theirs, theirs + 1, 1, 2, mine, mine + 1),
                    jnp.where(
                        middle, pick(0, 7, 1, 2, theirs, theirs + 1, mine, mine + 1),
                        jnp.where(
                            group == 1, pick(0, 1, 2, 7, mine, mine + 1, theirs, theirs + 1),
                            pick(0, 7, 1, 2, mine, mine + 1, theirs, theirs + 1),
                        ),
                    ),
                ),
            ),
        )
        for n, part in enumerate(parts):
            pl.when(what == n)(part)
        return carry

    lax.fori_loop(0, len(parts), turn, 0)

    @pl.when(seq == n_seq - 1)
    def _():
        ext[LEN : LEN + 8, :] = jnp.zeros((8, WIDTH), F32)

    cross = jnp.sum(ebuf[0] * ebuf[1], axis=0, keepdims=True)
    cross = by_head(jnp.broadcast_to(cross, (8, WIDTH)))[:, 0:1]
    col = col_s[...].T[0:HEADS, :]
    carried = carried_s[...]
    sgrad_ref[...] = col + to_end * carried
    lh, ll = split2(row_s[...] - col * step_t + from_start * read_s[...])
    eh, el = split2(to_end * step_t * carried)
    since = flag(rows >= cols)
    strict = flag(rows < cols)
    decay = dot(lh, since) + dot(ll, since) + dot(eh, strict) + dot(el, strict)
    dgrad_ref[...] = decay + jnp.exp(total) * cross

    def convolve(first, stop):
        acc = cw_ref[3:4, :] * ext[first:stop, :]
        for tap in range(3):
            acc = acc + cw_ref[tap : tap + 1, :] * ext[first + 3 - tap : stop + 3 - tap, :]
        igrad_ref[first:stop, :] = acc.astype(BF16)

    convolve(0, LEN - 16)

    k_copy.wait_send()
    q_copy.wait_send()
    d_copy.wait_send()
    for half in range(2):
        l_copy(half).wait_send()

    @pl.when(low)
    def _():
        dt_copy().wait_send()
        for c in range(CHUNKS):
            t_copy(c).wait_send()

    @pl.when(sends_on)
    def _():
        for c in range(CHUNKS):
            leaf_copy(c).wait_send()

    @pl.when(sends_far)
    def _():
        for c in range(CHUNKS):
            x_copy(c).wait_send()

    @pl.when(sends_last)
    def _():
        for c in range(CHUNKS):
            last_copy(c).wait_send()

    for c in range(CHUNKS):
        e_copy(c).wait_send()
    @pl.when(gives)
    def _():
        w_copy(group).wait_send()
        for p in range(CHUNKS // PIECE):
            u_copy(group, p).wait_send()

    @pl.when(gathers)
    def _():
        for c in range(CHUNKS):
            back_copy(c).wait_send()

    k_back.wait_recv()
    kgrad_ref[...] = k_in[...] + krecv[...].astype(F32)
    q_back.wait_recv()
    qgrad_ref[...] = q_in[...] + qrecv[...].astype(F32)

    pl.when(core == 0)(c_near.wait_recv)
    pl.when(takes_rows)(c_far.wait_recv)
    convolve(LEN - 16, LEN)

    k_back.wait_send()
    q_back.wait_send()

    @pl.when(core == 0)
    def _():
        for move in ahead:
            move.wait_send()

    pl.when(core == 1)(c_near.wait_send)
    pl.when(sends_rows)(c_far.wait_send)


def store_kernel(*refs):
    sems = refs[-1]
    moves = [pltpu.make_async_copy(refs[n], refs[n + 5], sems.at[n]) for n in range(5)]
    for move in moves:
        move.start()
    for move in moves:
        move.wait()


def body(n_seq, conv_output, output_grad, write_keys, read_queries, log_decay, step_size, skip_gain, conv_weight):
    shape = jax.ShapeDtypeStruct
    vmem = pltpu.VMEM
    dma = pltpu.SemaphoreType.DMA
    big = (STATE, WIDTH)
    tok = (LEN, WIDTH)
    sq = (LEN, LEN)
    small = (HEADS, LEN)
    row = (8, WIDTH)
    gmax = n_seq // 4 - 1
    in_vmem = pl.BlockSpec(memory_space=vmem)
    hbm = pl.BlockSpec(memory_space=pltpu.HBM)
    outs = (shape(tok, BF16), shape(sq, F32), shape(sq, F32), shape(small, F32), shape(small, F32))
    results = pl.pallas_call(
        functools.partial(kernel, n_seq),
        out_shape=tuple(vmem(o.shape, o.dtype) for o in outs),
        in_specs=[hbm] * 8,
        out_specs=(in_vmem,) * 5,
        scratch_shapes=[
            vmem(tok, BF16), vmem(tok, BF16), vmem(sq, BF16), vmem(sq, BF16),
            vmem(small, F32), vmem(small, F32), vmem((1, HEADS), F32), vmem((4, WIDTH), F32),
            vmem(sq, F32), vmem(sq, F32), vmem(small, F32), vmem(sq, BF16), vmem(sq, BF16),
            vmem(tok, BF16), vmem(tok, BF16), vmem(tok, F32), vmem(tok, F32), vmem(tok, F32),
            vmem(tok, BF16), vmem(tok, BF16), vmem(tok, BF16), vmem(tok, BF16), vmem(tok, F32),
            vmem(sq, F32), vmem(sq, F32), vmem(sq, F32), vmem(sq, F32), vmem(small, F32), vmem(small, F32),
            vmem(tok, F32), vmem(tok, F32),
            vmem(big, F32), vmem(big, F32), vmem(big, F32),
            vmem(big, F32), vmem(big, F32),
            vmem(row, F32), vmem(row, F32), vmem(row, F32), vmem(row, F32),
            vmem(big, F32), vmem(big, F32), vmem(big, BF16), vmem(big, BF16), vmem((2,) + big, F32), vmem(big, F32),
            vmem((LEN + 8, WIDTH), F32), vmem(sq, BF16), vmem(sq, BF16), vmem(sq, BF16), vmem(sq, BF16),
            vmem(row, F32), vmem(row, F32), vmem(row, F32), vmem(row, F32), vmem(row, F32),
            vmem((16, WIDTH), F32), vmem((16, LEN), BF16), vmem((16, LEN), BF16),
            vmem(big, BF16), vmem((gmax,) + big, BF16), vmem(row, F32), vmem((gmax,) + row, F32), vmem((8, WIDTH), F32),
            dma((8,)), dma((2,)), dma((2,)), dma((2,)), dma((2,)), dma((2,)), dma((2,)),
            dma((CHUNKS,)), dma((CHUNKS,)),
            dma((CHUNKS,)), dma((CHUNKS,)), dma((CHUNKS,)), dma((CHUNKS,)), dma((CHUNKS,)), dma((CHUNKS,)),
            dma((2,)), dma((2,)), dma((2,)), dma((2,)), dma((4,)), dma((4,)),
            dma((CHUNKS // PIECE,)), dma((gmax, CHUNKS // PIECE)), dma((1,)), dma((gmax,)),
        ],
        compiler_params=pltpu.CompilerParams(
            collective_id=0, has_side_effects=True, vmem_limit_bytes=VMEM_BYTES
        ),
        cost_estimate=pl.CostEstimate(flops=300_000_000, bytes_accessed=1_000_000, transcendentals=300_000),
    )(
        conv_output, output_grad, write_keys, read_queries, log_decay.T, step_size.T,
        skip_gain.reshape(1, HEADS), conv_weight,
    )
    igrad, kgrad, qgrad, dgrad, sgrad = pl.pallas_call(
        store_kernel,
        out_shape=outs,
        in_specs=[pl.BlockSpec(memory_space=pl.ANY)] * 5,
        out_specs=(hbm,) * 5,
        scratch_shapes=[dma((5,))],
        compiler_params=pltpu.CompilerParams(vmem_limit_bytes=16 * 1024 * 1024),
    )(*results)
    return igrad, kgrad, qgrad, dgrad.T, sgrad.T


def solution(mesh):
    spec = P("seq", "head")
    return jax.shard_map(
        functools.partial(body, mesh.shape["seq"]),
        mesh=mesh,
        in_specs=(spec, spec, spec, spec, spec, spec, P("head"), P(None, "head")),
        out_specs=(spec,) * 5,
        check_vma=False,
    )
```

```python
import functools

import jax
import jax.numpy as jnp
from jax import lax
from jax.experimental import pallas as pl
from jax.experimental.pallas import tpu as pltpu
from jax.sharding import PartitionSpec as P

MESH = pl.DeviceIdType.MESH
F32 = jnp.float32
BF16 = jnp.bfloat16
LEN = 128
WIDTH = 512
HEADS = 8
HALF = 128
VMEM_BYTES = 58000 * 1024
STATE = 256
CHUNK = 16
CHUNKS = STATE // CHUNK
NEAR_LAG = 6
PIECE = 4
HEAD_CHUNKS = HALF // 2 // CHUNK
FAR_DONE = CHUNKS - HEAD_CHUNKS


def dot(a, b):
    return lax.dot_general(a, b, (((1,), (0,)), ((), ())), preferred_element_type=F32)


def dot_t(a, b):
    return lax.dot_general(a, b, (((1,), (1,)), ((), ())), preferred_element_type=F32)


def split2(x):
    hi = x.astype(BF16)
    return hi, (x - hi.astype(F32)).astype(BF16)


def split3(x):
    hi = x.astype(BF16)
    rest = x - hi.astype(F32)
    mid = rest.astype(BF16)
    return hi, mid, (rest - mid.astype(F32)).astype(BF16)


def iota(shape, axis):
    return lax.broadcasted_iota(jnp.int32, shape, axis)


def flag(cond):
    return cond.astype(F32).astype(BF16)


def kernel(
    n_seq, conv_hbm, og_hbm, k_hbm, q_hbm, ld_hbm, ss_hbm, skip_hbm, cw_hbm,
    igrad_ref, kgrad_ref, qgrad_ref, dgrad_ref, sgrad_ref,
    conv_ref, og_ref, k_ref, q_ref, ld_ref, ss_ref, skip_ref, cw_ref,
    pack, col_s, row_s, kp, qp, vhi, vlo, vals, dsilu, tsx, whi, wlo, shi, slo, within,
    k_in, q_in, k_far, q_far, read_s, carried_s, out_acc, into_acc,
    lme, lsend, lother, tt, tlow, dme8, doth8, dchip8, dlow8, xin, xsend, xnear, xnsend, ebuf, epart,
    ext, kpart, qpart, krecv, qrecv, alpha, beta, alpha_r, beta_r, crow, crow16, k_top, kp_top, us, ubuf, dgroup8, dbuf, weight,
    in_s, kq_ss, kq_rs, d_ss, d_rs, l_ss, l_rs, t_ss, t_rs, x_ss, x2_ss, x_rs, n_rs, e_ss, e_rs, f_ss, f_rs, c_ss, c_rs, a_ss, a_rs,
    u_ss, u_rs, w_ss, w_rs,
):
    seq = lax.axis_index("seq")
    head = lax.axis_index("head")
    core = lax.rem(seq, 2)
    chip = seq // 2
    chips = n_seq // 2
    pos = jnp.where(core == 0, chip, chips - 1 - chip)
    group = pos // 2
    high = lax.rem(pos, 2) == 1
    low = lax.rem(pos, 2) == 0
    opens = group == 0
    late = group >= 3 * chips // 8
    middle = group >= chips // 4
    groups = chips // 2
    last_group = groups - 1 - core
    closes = group == last_group
    at_end = group == groups - 1
    backward = core == 1
    gathers = jnp.logical_and(backward, jnp.logical_and(high, at_end))
    gives = jnp.logical_and(backward, jnp.logical_and(high, group < groups - 1))
    gives_first = jnp.logical_and(gives, group >= 2)
    sends_on = jnp.logical_and(high, group < last_group)
    sends_last = jnp.logical_and(high, group == last_group - 1)
    sends_far = jnp.logical_and(high, group < last_group - 1)
    inner = jnp.logical_not(opens)
    takes32 = jnp.logical_and(inner, jnp.logical_and(high, jnp.logical_not(jnp.logical_or(closes, gathers))))
    takes16 = jnp.logical_and(inner, jnp.logical_or(low, closes))
    step1 = jnp.where(core == 0, 2, n_seq - 2)
    step2 = jnp.where(core == 0, 4, n_seq - 4)

    def at(s):
        return (lax.rem(s, n_seq), head)

    next1 = at(seq + step1)
    next2 = at(seq + step2)
    other_core = at(seq + 1 - 2 * core)
    partner = (seq, head + 1 - 2 * lax.rem(head, 2))

    barrier = pltpu.get_barrier_semaphore()
    near = (
        (seq + 2, chip < chips - 1), (seq + n_seq - 2, chip > 0), (seq + 4, chip < chips - 2), (seq + n_seq - 4, chip > 1),
    )
    greetings = jnp.int32(2)
    for peer, there in near:
        greetings = greetings + jnp.where(there, 1, 0)

        @pl.when(there)
        def _():
            pl.semaphore_signal(barrier, inc=1, device_id=at(peer), device_id_type=MESH)

    for peer in (other_core, partner):
        pl.semaphore_signal(barrier, inc=1, device_id=peer, device_id_type=MESH)

    moves = [
        pltpu.make_async_copy(src, dst, in_s.at[n])
        for n, (src, dst) in enumerate((
            (ld_hbm, ld_ref), (ss_hbm, ss_ref), (conv_hbm, conv_ref), (og_hbm, og_ref),
            (k_hbm, k_ref), (q_hbm, q_ref), (skip_hbm, skip_ref), (cw_hbm, cw_ref),
        ))
    ]
    for move in moves:
        move.start()

    def remote(src, dst, ss, rs, peer):
        return pltpu.make_async_remote_copy(
            src_ref=src, dst_ref=dst, send_sem=ss, recv_sem=rs, device_id=peer, device_id_type=MESH
        )

    @pl.when(gathers)
    def _():
        for z in range(4, chips, 2):
            pl.semaphore_signal(barrier, inc=1, device_id=(2 * z + 1, head), device_id_type=MESH)

    far_giver = jnp.logical_and(gives, chip >= 4)
    pl.semaphore_wait(barrier, greetings + jnp.where(far_giver, 1, 0))

    k_copy = remote(k_hbm, kp, kq_ss.at[0], kq_rs.at[0], partner)
    q_copy = remote(q_hbm, qp, kq_ss.at[1], kq_rs.at[1], partner)
    k_copy.start()
    q_copy.start()

    rows = iota((LEN, LEN), 0)
    cols = iota((LEN, LEN), 1)
    upto = flag(rows <= cols)
    pack[...] = jnp.zeros((LEN, LEN), F32)
    heads_rows = flag(iota((HEADS, WIDTH), 0) == iota((HEADS, WIDTH), 1) // 64)

    def spread(base):
        return flag(iota((LEN, WIDTH), 0) - base == iota((LEN, WIDTH), 1) // 64)

    def by_head(x):
        hi, lo = split2(x)
        return dot_t(heads_rows, hi) + dot_t(heads_rows, lo)

    moves[0].wait()
    moves[1].wait()
    hi, mid, lo = split3(ld_ref[...])
    cum_t = dot(hi, upto) + (dot(mid, upto) + dot(lo, upto))
    step_t = ss_ref[...]
    total = cum_t[:, LEN - 1 : LEN]
    from_start = jnp.exp(cum_t)
    to_end = jnp.exp(total - cum_t)
    pack[0:8, :] = cum_t
    pack[8:16, :] = step_t
    pack[16:24, :] = from_start
    pack[24:32, :] = to_end * step_t
    columns = pack[...].T
    c_hi, c_lo = split2(columns)
    fs_sel, ts_sel = spread(16), spread(24)
    fsx = dot(c_hi, fs_sel) + dot(c_lo, fs_sel)
    tsx[...] = dot(c_hi, ts_sel) + dot(c_lo, ts_sel)
    dme8[...] = jnp.broadcast_to(fsx[LEN - 1 : LEN, :], (8, WIDTH))

    d_copy = remote(dme8, doth8, d_ss.at[0], d_rs.at[0], other_core)
    d_copy.start()

    moves[2].wait()
    preact = conv_ref[...].astype(F32)
    sig = 1.0 / (1.0 + jnp.exp(-preact))
    value = preact * sig
    vals[...] = value
    vhi[...], vlo[...] = split2(value)
    dsilu[...] = sig * (1.0 + preact * (1.0 - sig))
    whi[...], wlo[...] = split2(value * tsx[...])
    moves[3].wait()
    shi[...], slo[...] = split2(og_ref[...].astype(F32) * fsx)

    forward = core == 0

    def turned(x):
        return x.astype(F32).T.astype(BF16)

    def l_copy(half):
        part = pl.ds(half * HALF, HALF)
        return remote(lsend.at[part], lother.at[part], l_ss.at[half], l_rs.at[half], other_core)

    def local_half(half, kk, qq):
        sl = slice(half * HALF, half * HALF + HALF)
        kt, qt = turned(kk), turned(qq)
        wh, wl, sh, slw = whi[...], wlo[...], shi[...], slo[...]
        mine, other = jnp.where(forward, kt, qt), jnp.where(forward, qt, kt)
        lsend[sl, :] = dot(other, jnp.where(forward, sh, wh)) + dot(other, jnp.where(forward, slw, wl))
        l_copy(half).start()
        lme[sl, :] = dot(mine, jnp.where(forward, wh, sh)) + dot(mine, jnp.where(forward, wl, slw))

    moves[4].wait()
    moves[5].wait()
    local_half(0, k_ref[...], q_ref[...])
    k_copy.wait_recv()
    q_copy.wait_recv()
    local_half(1, kp[...], qp[...])
    moves[6].wait()
    moves[7].wait()

    d_copy.wait_recv()
    dchip8[...] = dme8[...] * doth8[...]

    def first_row(c):
        if c < HEAD_CHUNKS:
            return c * CHUNK
        if c < FAR_DONE:
            return HALF + (c - HEAD_CHUNKS) * CHUNK
        return (c - HALF // CHUNK) * CHUNK

    def dt_copy():
        return remote(dchip8, dlow8, d_ss.at[1], d_rs.at[1], next1)

    def t_copy(c):
        part = pl.ds(first_row(c), CHUNK)
        return remote(tt.at[part], tlow.at[part], t_ss.at[c], t_rs.at[c], next1)

    @pl.when(low)
    def _():
        dt_copy().start()

    for c in range(CHUNKS):
        sl = slice(first_row(c), first_row(c) + CHUNK)
        if c == 0:
            l_copy(0).wait_recv()
        if c == HEAD_CHUNKS:
            l_copy(1).wait_recv()
        tt[sl, :] = doth8[0:1, :] * lme[sl, :] + lother[sl, :]

        @pl.when(low)
        def _():
            t_copy(c).start()

    @pl.when(low)
    def _():
        tlow[...] = jnp.zeros((STATE, WIDTH), F32)
        dlow8[...] = jnp.ones((8, WIDTH), F32)

    @pl.when(opens)
    def _():
        xin[...] = jnp.zeros((STATE, WIDTH), F32)

    def x_copy(c):
        part = pl.ds(first_row(c), CHUNK)
        return remote(xsend.at[part], xin.at[part], x2_ss.at[c], x_rs.at[c], next2)

    def leaf_copy(c):
        part = pl.ds(first_row(c), CHUNK)
        return remote(xnsend.at[part], xnear.at[part], x_ss.at[c], n_rs.at[c], next1)

    def u_copy(g, p):
        part = pl.ds(first_row(p * PIECE), PIECE * CHUNK)
        return remote(us.at[part], ubuf.at[g, part], u_ss.at[p], u_rs.at[g, p], (1, head))

    def w_copy(g):
        return remote(dgroup8, dbuf.at[g], w_ss.at[0], w_rs.at[g], (1, head))

    def back_copy(c):
        part = pl.ds(first_row(c), CHUNK)
        return remote(xnsend.at[part], xnear.at[part], x_ss.at[c], n_rs.at[c], at(seq + 2))

    def give():
        @pl.when(gives)
        def _():
            @pl.when(gives_first)
            def _():
                dt_copy().wait_recv()

            dchip = dchip8[0:1, :]
            dgroup8[...] = dchip8[...] * dlow8[...]
            w_copy(group).start()
            for p in range(CHUNKS // PIECE):
                @pl.when(gives_first)
                def _():
                    for c in range(p * PIECE, p * PIECE + PIECE):
                        t_copy(c).wait_recv()

                sl = slice(first_row(p * PIECE), first_row(p * PIECE) + PIECE * CHUNK)
                us[sl, :] = (dchip * tlow[sl, :] + tt[sl, :]).astype(BF16)
                u_copy(group, p).start()

    def last_copy(c):
        part = pl.ds(first_row(c), CHUNK)
        return remote(xnsend.at[part], xnear.at[part], x2_ss.at[c], n_rs.at[c], next2)

    def e_copy(c):
        part = pl.ds(first_row(c), CHUNK)
        return remote(epart.at[part], ebuf.at[core, part], e_ss.at[c], e_rs.at[c], other_core)

    def chain(half):
        if half == 0:

            @pl.when(jnp.logical_and(high, jnp.logical_not(gives_first)))
            def _():
                dt_copy().wait_recv()

            @pl.when(gathers)
            def _():
                for g in range(groups - 1):
                    w_copy(g).wait_recv()
                share = jnp.ones((1, WIDTH), F32)
                for g in range(groups - 2, -1, -1):
                    weight[g : g + 1, :] = share
                    share = share * dbuf[g, 0:1, :]

        a = dlow8[0:1, :]
        dchip = dchip8[0:1, :]
        dd = dchip * a
        dm = dme8[0:1, :]

        def forward_chunk(c):
            sl = slice(first_row(c), first_row(c) + CHUNK)

            @pl.when(jnp.logical_and(high, jnp.logical_not(gives_first)))
            def _():
                t_copy(c).wait_recv()

            @pl.when(gathers)
            def _():
                if c % PIECE == 0:
                    for g in range(groups - 1):
                        u_copy(g, c // PIECE).wait_recv()
                x = weight[0:1, :] * ubuf[0, sl, :].astype(F32)
                for g in range(1, groups - 1):
                    x = x + weight[g : g + 1, :] * ubuf[g, sl, :].astype(F32)
                xin[sl, :] = x
                xnsend[sl, :] = x.astype(BF16)
                back_copy(c).start()

            @pl.when(takes32)
            def _():
                x_copy(c).wait_recv()

            @pl.when(takes16)
            def _():
                leaf_copy(c).wait_recv()
                xin[sl, :] = xnear[sl, :].astype(F32)

            @pl.when(sends_far)
            def _():
                x = dd * xin[sl, :] + (dchip * tlow[sl, :] + tt[sl, :])
                xsend[sl, :] = x
                x_copy(c).start()
                xnsend[sl, :] = x.astype(BF16)

            @pl.when(sends_last)
            def _():
                x = dd * xin[sl, :] + (dchip * tlow[sl, :] + tt[sl, :])
                xnsend[sl, :] = x.astype(BF16)
                last_copy(c).start()
                leaf_copy(c).start()

        def use_chunk(c):
            sl = slice(first_row(c), first_row(c) + CHUNK)
            em = a * xin[sl, :] + tlow[sl, :]
            ebuf[core, sl, :] = em
            epart[sl, :] = dm * em + lme[sl, :]
            e_copy(c).start()

        start, stop = (0, FAR_DONE) if half == 0 else (FAR_DONE, CHUNKS)
        for c in range(start, stop):
            forward_chunk(c)
            if c >= NEAR_LAG:
                pl.when(sends_far)(leaf_copy(c - NEAR_LAG).start)
            if c > start:
                use_chunk(c - 1)
        if half == 1:

            @pl.when(sends_far)
            def _():
                for c in range(CHUNKS - NEAR_LAG, CHUNKS):
                    leaf_copy(c).start()

        use_chunk(stop - 1)

    ahead = [
        remote(src, dst, a_ss.at[n], a_rs.at[n], other_core)
        for n, (src, dst) in enumerate((
            (alpha, alpha_r), (beta, beta_r), (k_ref.at[pl.ds(0, 16)], k_top), (kp.at[pl.ds(0, 16)], kp_top),
        ))
    ]

    def inside():
        scores = dot_t(k_ref[...], q_ref[...]) + dot_t(kp[...], qp[...])
        causal = rows <= cols
        left = iota((LEN, LEN), 1) < 64
        col_s[...] = jnp.zeros((LEN, LEN), F32)
        weights = jnp.zeros((LEN, LEN), F32)
        for j in range(HEADS // 2):
            lanes = slice(j * 128, j * 128 + 128)
            ogb = og_ref[:, lanes]
            vh, vl = vhi[:, lanes], vlo[:, lanes]
            none = jnp.zeros_like(vh)
            halves = []
            for e in range(2):
                h = 2 * j + e
                own = left if e == 0 else jnp.logical_not(left)
                pd = dot_t(jnp.where(own, vh, none), ogb) + dot_t(jnp.where(own, vl, none), ogb)
                gap = cum_t[h : h + 1, :] - columns[:, h : h + 1]
                dm = jnp.exp(jnp.where(causal, gap, -1e30))
                st = columns[:, 8 + h : 9 + h]
                dm_st = dm * st
                weights = weights + dm_st * pd
                eff = dm * scores * pd
                col_s[:, h : h + 1] = jnp.sum(eff, axis=1, keepdims=True)
                row_s[h : h + 1, :] = jnp.sum(eff * st, axis=0, keepdims=True)
                halves.append(dot((dm_st * scores).astype(BF16), ogb))
            within[:, lanes] = jnp.where(left, halves[0], halves[1])
        w16 = weights.astype(BF16)
        w16_t = weights.T.astype(BF16)
        k_far[...] = dot(w16, qp[...])
        q_far[...] = dot(w16_t, kp[...])
        k_in[...] = dot(w16, q_ref[...])
        q_in[...] = dot(w16_t, k_ref[...])
        skips = jnp.broadcast_to(skip_ref[...], (LEN, HEADS))
        sk_hi, sk_lo = split2(skips)
        skip_row = (dot(sk_hi, heads_rows) + dot(sk_lo, heads_rows))[0:1, :]
        within[...] = within[...] + skip_row * og_ref[...].astype(F32)
        alpha[...] = within[0:8, :] * dsilu[0:8, :]
        beta[...] = tsx[0:8, :] * dsilu[0:8, :]

        @pl.when(core == 0)
        def _():
            for move in ahead:
                move.start()

    k_back = remote(kpart, krecv, f_ss.at[0], f_rs.at[0], partner)
    q_back = remote(qpart, qrecv, f_ss.at[1], f_rs.at[1], partner)
    c_far = remote(crow, ext.at[pl.ds(LEN, 8)], c_ss.at[0], c_rs.at[0], next1)
    c_near = remote(ext.at[pl.ds(0, 8)], ext.at[pl.ds(LEN, 8)], c_ss.at[1], c_rs.at[1], other_core)
    sends_rows = jnp.logical_and(core == 1, chip > 0)
    takes_rows = jnp.logical_and(core == 1, chip < chips - 1)

    def both(a, b):
        return dot(a, b[0]) + dot(a, b[1])

    def their_chunks(of_core, half):
        @pl.when(core == of_core)
        def _():
            for c in range(0, FAR_DONE) if half == 0 else range(FAR_DONE, CHUNKS):
                e_copy(c).wait_recv()

    def entering_far():
        their_chunks(1, 0)
        far = split2(ebuf[0, HALF:, :])
        qpart[...] = (q_far[...] + dot_t(shi[...], far[0])).astype(BF16)
        q_back.start()
        out_acc[...] = both(qp[...], far)

    def entering_own():
        their_chunks(1, 1)
        own = split2(ebuf[0, 0:HALF, :])
        out_of = out_acc[...] + both(q_ref[...], own)
        read_s[...] = by_head(og_ref[...].astype(F32) * out_of)
        q_in[...] = q_in[...] + dot_t(shi[...], own[0])

    def arriving_far():
        their_chunks(0, 0)
        far = split2(ebuf[1, HALF:, :])
        kpart[...] = (k_far[...] + dot_t(whi[...], far[0])).astype(BF16)
        k_back.start()
        into_acc[...] = both(kp[...], far)

        @pl.when(core == 1)
        def _():
            for move in ahead:
                move.wait_recv()
            crow16[...] = both(kp_top[...], split2(epart[HALF:, :]))

    def convolve(first, stop):
        acc = cw_ref[3:4, :] * ext[first:stop, :]
        for tap in range(3):
            acc = acc + cw_ref[tap : tap + 1, :] * ext[first + 3 - tap : stop + 3 - tap, :]
        igrad_ref[first:stop, :] = acc.astype(BF16)

    def arriving_own():
        their_chunks(0, 1)
        own = split2(ebuf[1, 0:HALF, :])

        @pl.when(core == 1)
        def _():
            rows_of = both(k_top[...], split2(epart[0:HALF, :])) + crow16[...]
            crow[...] = alpha_r[...] + beta_r[...] * rows_of[0:8, :]
            pl.when(sends_rows)(c_far.start)

        into = into_acc[...] + both(k_ref[...], own)
        ext[0:LEN, :] = (within[...] + tsx[...] * into) * dsilu[...]
        pl.when(core == 1)(c_near.start)
        carried_s[...] = by_head(vals[...] * into)
        k_in[...] = k_in[...] + dot_t(whi[...], own[0])
        convolve(0, LEN - 16)

    parts = (
        inside, functools.partial(chain, 0), functools.partial(chain, 1),
        entering_far, entering_own, arriving_far, arriving_own, give,
    )
    mine = jnp.where(forward, 3, 5)
    theirs = 8 - mine

    def turn(i, carry):
        def pick(*order):
            what = jnp.int32(0)
            for n, part in enumerate(order):
                what = jnp.where(i == n, part, what)
            return what

        what = jnp.where(
            opens, pick(1, 2, 7, 0, mine, mine + 1, theirs, theirs + 1),
            jnp.where(
                jnp.logical_or(closes, jnp.logical_and(at_end, jnp.logical_not(gathers))), pick(0, 7, theirs, theirs + 1, 1, mine, 2, mine + 1),
                jnp.where(
                    late, pick(0, 7, theirs, theirs + 1, 1, 2, mine, mine + 1),
                    jnp.where(
                        middle, pick(0, 7, 1, 2, theirs, theirs + 1, mine, mine + 1),
                        jnp.where(
                            group == 1, pick(0, 1, 2, 7, mine, mine + 1, theirs, theirs + 1),
                            pick(0, 7, 1, 2, mine, mine + 1, theirs, theirs + 1),
                        ),
                    ),
                ),
            ),
        )
        for n, part in enumerate(parts):
            pl.when(what == n)(part)
        return carry

    lax.fori_loop(0, len(parts), turn, 0)

    @pl.when(seq == n_seq - 1)
    def _():
        ext[LEN : LEN + 8, :] = jnp.zeros((8, WIDTH), F32)

    cross = jnp.sum(ebuf[0] * ebuf[1], axis=0, keepdims=True)
    cross = by_head(jnp.broadcast_to(cross, (8, WIDTH)))[:, 0:1]
    col = col_s[...].T[0:HEADS, :]
    carried = carried_s[...]
    sgrad_ref[...] = col + to_end * carried
    lh, ll = split2(row_s[...] - col * step_t + from_start * read_s[...])
    eh, el = split2(to_end * step_t * carried)
    since = flag(rows >= cols)
    strict = flag(rows < cols)
    decay = dot(lh, since) + dot(ll, since) + dot(eh, strict) + dot(el, strict)
    dgrad_ref[...] = decay + jnp.exp(total) * cross

    k_copy.wait_send()
    q_copy.wait_send()
    d_copy.wait_send()
    for half in range(2):
        l_copy(half).wait_send()

    @pl.when(low)
    def _():
        dt_copy().wait_send()
        for c in range(CHUNKS):
            t_copy(c).wait_send()

    @pl.when(sends_on)
    def _():
        for c in range(CHUNKS):
            leaf_copy(c).wait_send()

    @pl.when(sends_far)
    def _():
        for c in range(CHUNKS):
            x_copy(c).wait_send()

    @pl.when(sends_last)
    def _():
        for c in range(CHUNKS):
            last_copy(c).wait_send()

    for c in range(CHUNKS):
        e_copy(c).wait_send()
    @pl.when(gives)
    def _():
        w_copy(group).wait_send()
        for p in range(CHUNKS // PIECE):
            u_copy(group, p).wait_send()

    @pl.when(gathers)
    def _():
        for c in range(CHUNKS):
            back_copy(c).wait_send()

    k_back.wait_recv()
    kgrad_ref[...] = k_in[...] + krecv[...].astype(F32)
    q_back.wait_recv()
    qgrad_ref[...] = q_in[...] + qrecv[...].astype(F32)

    pl.when(core == 0)(c_near.wait_recv)
    pl.when(takes_rows)(c_far.wait_recv)
    convolve(LEN - 16, LEN)

    k_back.wait_send()
    q_back.wait_send()

    @pl.when(core == 0)
    def _():
        for move in ahead:
            move.wait_send()

    pl.when(core == 1)(c_near.wait_send)
    pl.when(sends_rows)(c_far.wait_send)


def store_kernel(*refs):
    sems = refs[-1]
    moves = [pltpu.make_async_copy(refs[n], refs[n + 5], sems.at[n]) for n in range(5)]
    for move in moves:
        move.start()
    for move in moves:
        move.wait()


def body(n_seq, conv_output, output_grad, write_keys, read_queries, log_decay, step_size, skip_gain, conv_weight):
    shape = jax.ShapeDtypeStruct
    vmem = pltpu.VMEM
    dma = pltpu.SemaphoreType.DMA
    big = (STATE, WIDTH)
    tok = (LEN, WIDTH)
    sq = (LEN, LEN)
    small = (HEADS, LEN)
    row = (8, WIDTH)
    gmax = n_seq // 4 - 1
    in_vmem = pl.BlockSpec(memory_space=vmem)
    hbm = pl.BlockSpec(memory_space=pltpu.HBM)
    outs = (shape(tok, BF16), shape(sq, F32), shape(sq, F32), shape(small, F32), shape(small, F32))
    results = pl.pallas_call(
        functools.partial(kernel, n_seq),
        out_shape=tuple(vmem(o.shape, o.dtype) for o in outs),
        in_specs=[hbm] * 8,
        out_specs=(in_vmem,) * 5,
        scratch_shapes=[
            vmem(tok, BF16), vmem(tok, BF16), vmem(sq, BF16), vmem(sq, BF16),
            vmem(small, F32), vmem(small, F32), vmem((1, HEADS), F32), vmem((4, WIDTH), F32),
            vmem(sq, F32), vmem(sq, F32), vmem(small, F32), vmem(sq, BF16), vmem(sq, BF16),
            vmem(tok, BF16), vmem(tok, BF16), vmem(tok, F32), vmem(tok, F32), vmem(tok, F32),
            vmem(tok, BF16), vmem(tok, BF16), vmem(tok, BF16), vmem(tok, BF16), vmem(tok, F32),
            vmem(sq, F32), vmem(sq, F32), vmem(sq, F32), vmem(sq, F32), vmem(small, F32), vmem(small, F32),
            vmem(tok, F32), vmem(tok, F32),
            vmem(big, F32), vmem(big, F32), vmem(big, F32),
            vmem(big, F32), vmem(big, F32),
            vmem(row, F32), vmem(row, F32), vmem(row, F32), vmem(row, F32),
            vmem(big, F32), vmem(big, F32), vmem(big, BF16), vmem(big, BF16), vmem((2,) + big, F32), vmem(big, F32),
            vmem((LEN + 8, WIDTH), F32), vmem(sq, BF16), vmem(sq, BF16), vmem(sq, BF16), vmem(sq, BF16),
            vmem(row, F32), vmem(row, F32), vmem(row, F32), vmem(row, F32), vmem(row, F32),
            vmem((16, WIDTH), F32), vmem((16, LEN), BF16), vmem((16, LEN), BF16),
            vmem(big, BF16), vmem((gmax,) + big, BF16), vmem(row, F32), vmem((gmax,) + row, F32), vmem((8, WIDTH), F32),
            dma((8,)), dma((2,)), dma((2,)), dma((2,)), dma((2,)), dma((2,)), dma((2,)),
            dma((CHUNKS,)), dma((CHUNKS,)),
            dma((CHUNKS,)), dma((CHUNKS,)), dma((CHUNKS,)), dma((CHUNKS,)), dma((CHUNKS,)), dma((CHUNKS,)),
            dma((2,)), dma((2,)), dma((2,)), dma((2,)), dma((4,)), dma((4,)),
            dma((CHUNKS // PIECE,)), dma((gmax, CHUNKS // PIECE)), dma((1,)), dma((gmax,)),
        ],
        compiler_params=pltpu.CompilerParams(
            collective_id=0, has_side_effects=True, vmem_limit_bytes=VMEM_BYTES
        ),
        cost_estimate=pl.CostEstimate(flops=300_000_000, bytes_accessed=1_000_000, transcendentals=300_000),
    )(
        conv_output, output_grad, write_keys, read_queries, log_decay.T, step_size.T,
        skip_gain.reshape(1, HEADS), conv_weight,
    )
    igrad, kgrad, qgrad, dgrad, sgrad = pl.pallas_call(
        store_kernel,
        out_shape=outs,
        in_specs=[pl.BlockSpec(memory_space=pl.ANY)] * 5,
        out_specs=(hbm,) * 5,
        scratch_shapes=[dma((5,))],
        compiler_params=pltpu.CompilerParams(vmem_limit_bytes=16 * 1024 * 1024),
    )(*results)
    return igrad, kgrad, qgrad, dgrad.T, sgrad.T


def solution(mesh):
    spec = P("seq", "head")
    return jax.shard_map(
        functools.partial(body, mesh.shape["seq"]),
        mesh=mesh,
        in_specs=(spec, spec, spec, spec, spec, spec, P("head"), P(None, "head")),
        out_specs=(spec,) * 5,
        check_vma=False,
    )
```
